128 devices in a mesh: gx: 4 (over z), gy: 4 (over x_hi, core), gz: 8 (over y, x_lo).
Axes of the slice: x: 4 (x_hi: 2, x_lo: 2; x = x_hi * 2 + x_lo), y: 4, z: 4, core: 2. Of those that a mesh axis runs over, the one named last changes fastest.
Arguments:
- particles: float32 [7, 4, 4, 8, 49152], P(None, 'gx', 'gy', 'gz'), may hold values from -3.5 to 8, as said below
- labels: int32 [4, 4, 8, 49152], P('gx', 'gy', 'gz'), may hold values from 0 to 4096, as said below
- member_slot: int32 [4, 4, 8, 49152], P('gx', 'gy', 'gz'), may hold values from 0 to 31, as said below
- owner_slot: int32 [4096], replicated, may hold values from 0 to 4095, as said below
Outputs:
- edge_potential: float32 [4, 4, 8, 49152], P('gx', 'gy', 'gz')
- group_energy: float32 [4, 4, 8, 49152], P('gx', 'gy', 'gz')
The draws below stay inside these ranges and needn't reach their ends.
Inputs may be any that keep to these rules, and one draw needn't show every extreme that they name: `labels`: A domain gives at most 32 members to one group; the owner's own domain gives exactly 32 members to each of its groups. A group's members lie in domains whose coordinates differ from its owner's by d with d in -1, 0, 1 along each axis, d taken as in the statement. `member_slot`: the members of one domain in one group hold places 0 to c - 1 without repeats; particles in no group hold 0. `owner_slot`: A permutation: each domain owns exactly 32 groups. `particles`: positions lie in 0 to 8 within their own face tile; velocities lie in -3.5 to 3.5; masses are positive.
All inputs are finite; a program needn't handle non-finite values.
Results may differ from the reference program's by a relative error of at most 0.00018.
Values sent between devices are 32-bit elements; how exact they have to be, the bound alone decides.
No kernel may reach another device: no remote copies, remote signals or barrier semaphores. Data moves between devices by JAX's collectives and lax.ppermute only.
A program may use at most 128 MiB of HBM per device.

```python
import math
import jax
import jax.numpy as jnp
from jax import lax

TG = 8
GROUPS_DEV = 32
GCAP = 32
SLAB = 8192
DOMAINS = 128
NGROUPS = 4096
N_GX = 4
N_GY = 4
N_GZ = 8


def owner_tables(key):
    key_perm = jax.random.fold_in(key, 11)
    key_heavy = jax.random.fold_in(key, 13)
    owner_order = jax.random.permutation(key_perm, NGROUPS).astype(jnp.int32)
    heavy_rank = jax.random.permutation(key_heavy, DOMAINS)
    return (owner_order, heavy_rank < DOMAINS // 8)


def canonical(step, count):
    return (step + count // 2) % count - count // 2 == step


def member_tables(key):
    owner_order, heavy_device = owner_tables(key)
    key_members = jax.random.fold_in(key, 17)
    key_heavy, key_light, key_place = jax.random.split(key_members, 3)
    slab_all = 6 * SLAB
    group_at = jnp.zeros((NGROUPS,), jnp.int32).at[owner_order].set(jnp.arange(NGROUPS, dtype=jnp.int32))
    source = jnp.arange(DOMAINS, dtype=jnp.int32)
    cell_x = (source // (N_GY * N_GZ))[:, None]
    cell_y = (source // N_GZ % N_GY)[:, None]
    cell_z = (source % N_GZ)[:, None]
    offsets = jnp.arange(27, dtype=jnp.int32)
    step_x = (offsets // 9 - 1)[None, :]
    step_y = (offsets // 3 % 3 - 1)[None, :]
    step_z = (offsets % 3 - 1)[None, :]
    valid = canonical(step_x, N_GX) & canonical(step_y, N_GY) & canonical(step_z, N_GZ)
    owner = ((cell_x - step_x) % N_GX * N_GY + (cell_y - step_y) % N_GY) * N_GZ + (cell_z - step_z) % N_GZ
    heavy = heavy_device[owner][:, :, None]
    heavy_count = jax.random.randint(key_heavy, (DOMAINS, 27, GROUPS_DEV), 3 * GCAP // 4, GCAP + 1)
    light_count = jax.random.randint(key_light, (DOMAINS, 27, GROUPS_DEV), GCAP // 4, GCAP // 2 + 1)
    counts = jnp.where(heavy, heavy_count, light_count)
    counts = jnp.where((offsets == 13)[None, :, None], GCAP, counts)
    counts = jnp.where(valid[:, :, None], counts, 0).astype(jnp.int32)
    positions = jnp.arange(GCAP, dtype=jnp.int32)
    is_live = (positions[None, None, None, :] < counts[:, :, :, None]).reshape(DOMAINS, 27 * GROUPS_DEV * GCAP)
    live_rank = jnp.cumsum(is_live.astype(jnp.int32), axis=1) - 1
    orders = jax.vmap(lambda one_key: jax.random.permutation(one_key, slab_all))(jax.random.split(key_place, DOMAINS)).astype(jnp.int32)
    placed = jnp.take_along_axis(orders, jnp.clip(live_rank, 0, slab_all - 1), axis=1)
    placed = jnp.where(is_live, placed, slab_all)
    group_ids = group_at[owner[:, :, None] * GROUPS_DEV + jnp.arange(GROUPS_DEV, dtype=jnp.int32)[None, None, :]]
    entry_group = jnp.broadcast_to(group_ids[:, :, :, None], (DOMAINS, 27, GROUPS_DEV, GCAP)).reshape(placed.shape)
    entry_slot = jnp.broadcast_to(positions[None, None, None, :], (DOMAINS, 27, GROUPS_DEV, GCAP)).reshape(placed.shape)
    row_index = jnp.broadcast_to(jnp.arange(DOMAINS, dtype=jnp.int32)[:, None], placed.shape)
    label_table = jnp.full((DOMAINS, slab_all), NGROUPS, jnp.int32).at[row_index, placed].set(entry_group, mode='drop')
    slot_table = jnp.zeros((DOMAINS, slab_all), jnp.int32).at[row_index, placed].set(entry_slot, mode='drop')
    return (label_table.reshape(N_GX, N_GY, N_GZ, slab_all), slot_table.reshape(N_GX, N_GY, N_GZ, slab_all))


def draw_labels(key, part):
    label_table, slot_table = member_tables(key)
    return label_table


def draw_member_slot(key, part):
    label_table, slot_table = member_tables(key)
    return slot_table


def draw_owner_slot(key, part):
    owner_order, heavy_device = owner_tables(key)
    return owner_order


def draw_particles(key, part):
    key = jax.random.fold_in(key, 7)
    key_pos, key_vel, key_mass = jax.random.split(key, 3)
    tiles_face = TG * TG
    draw_shape = (N_GX, N_GY, N_GZ, 6, tiles_face, 128)
    face_id = jnp.arange(6)[:, None, None]
    tile_id = jnp.arange(tiles_face)[None, :, None]
    first_index = (tile_id // TG).astype(jnp.float32)
    second_index = (tile_id % TG).astype(jnp.float32)
    axis_of_face = face_id // 2
    high_side = (face_id % 2).astype(jnp.float32)
    jitter = jax.random.uniform(key_pos, (3,) + draw_shape)
    components = []
    for component in range(3):
        across = jnp.where(component < axis_of_face, component, component - 1)
        offset_base = jnp.where(across == 0, first_index, second_index)
        offset_base = jnp.where(axis_of_face == component, high_side * (TG - 1), offset_base)
        components.append(offset_base + jitter[component])
    velocity = jnp.clip(jax.random.normal(key_vel, (3,) + draw_shape), -3.5, 3.5)
    masses = jnp.exp(jax.random.uniform(key_mass, draw_shape, minval=math.log(0.5), maxval=math.log(2.0)))
    stacked = jnp.stack(components + [velocity[0], velocity[1], velocity[2], masses], axis=0)
    return stacked.reshape(7, N_GX, N_GY, N_GZ, 6 * tiles_face * 128)


def setup_inputs(seed: int = 0) -> dict:
    keys = jax.random.split(jax.random.key(seed), 5)
    particles = draw_particles(jax.random.fold_in(keys[4], 71), 0)
    labels = draw_labels(jax.random.fold_in(keys[4], 71), 0)
    member_slot = draw_member_slot(jax.random.fold_in(keys[4], 71), 0)
    owner_slot = draw_owner_slot(jax.random.fold_in(keys[4], 71), 0)
    return dict(particles=particles, labels=labels, member_slot=member_slot, owner_slot=owner_slot)


SOFTENING = 0.01
EDGE_COUPLING = 1.0 / 256.0
GROUP_COUPLING = 1.0 / 16.0

def tile_potential(targets, sources, exclude):
    squared = (targets[0][:, :, None] - sources[0][:, None, :]) ** 2
    squared = squared + (targets[1][:, :, None] - sources[1][:, None, :]) ** 2
    squared = squared + (targets[2][:, :, None] - sources[2][:, None, :]) ** 2
    weighted = sources[3][:, None, :] * lax.rsqrt(squared + SOFTENING)
    if exclude:
        diagonal = jnp.eye(targets.shape[2], dtype=jnp.bool_)
        weighted = jnp.where(diagonal[None], 0.0, weighted)
    return lax.optimization_barrier(jnp.sum(weighted, axis=2))

def group_energy_block(block_data):
    masses = block_data[6]
    total_mass = lax.optimization_barrier(jnp.sum(masses, axis=1))
    kinetic = jnp.zeros_like(masses)
    for component in range(3):
        velocity = block_data[3 + component]
        mean_velocity = lax.optimization_barrier(jnp.sum(masses * velocity, axis=1)) / total_mass
        kinetic = kinetic + (velocity - mean_velocity[:, None]) ** 2
    sources = jnp.concatenate([block_data[0:3], block_data[6:7]], axis=0)
    potential = tile_potential(block_data[0:3], sources, True)
    return -GROUP_COUPLING * potential + 0.5 * kinetic

def wrapped_step(source_cell, owner_cell, count):
    return ((source_cell - owner_cell + count // 2) % count - count // 2).astype(jnp.int32)

def reference(particles, labels, member_slot, owner_slot):
    domains = N_GX * N_GY * N_GZ
    ngroups = owner_slot.shape[0]
    slab_all = particles.shape[-1]
    tile_data = particles.reshape(7, N_GX, N_GY, N_GZ, 6, TG * TG, 128)
    carried = jnp.concatenate([tile_data[0:3], tile_data[6:7]], axis=0)
    ghost_faces = []
    for axis_id in range(3):
        from_lower = jnp.roll(carried[:, :, :, :, 2 * axis_id + 1], 1, axis=1 + axis_id)
        from_upper = jnp.roll(carried[:, :, :, :, 2 * axis_id], -1, axis=1 + axis_id)
        ghost_faces.append(from_lower.at[axis_id].add(-1.0 * TG))
        ghost_faces.append(from_upper.at[axis_id].add(1.0 * TG))
    ghosts = jnp.stack(ghost_faces, axis=4)
    own_flat = jnp.moveaxis(carried.reshape(4, domains, 6 * TG * TG, 128), 1, 0)
    ghost_flat = jnp.moveaxis(ghosts.reshape(4, domains, 6 * TG * TG, 128), 1, 0)

    def device_edge(inputs):
        own_tiles, ghost_tiles = inputs
        near = tile_potential(own_tiles[0:3], own_tiles, True)
        far = tile_potential(own_tiles[0:3], ghost_tiles, False)
        return -EDGE_COUPLING * (near + far)
    edge_potential = lax.map(device_edge, (own_flat, ghost_flat)).reshape(N_GX, N_GY, N_GZ, slab_all)
    flat_labels = labels.reshape(domains, slab_all)
    flat_slots = member_slot.reshape(domains, slab_all)
    member = flat_labels < ngroups
    safe_label = jnp.where(member, flat_labels, 0).astype(jnp.int32)
    owner_device = owner_slot[safe_label] // GROUPS_DEV
    source_device = jnp.arange(domains, dtype=jnp.int32)[:, None]
    flat_parts = particles.reshape(7, domains, slab_all)
    coordinates = []
    offset_index = jnp.zeros(flat_labels.shape, jnp.int32)
    strides = [(N_GY * N_GZ, N_GX), (N_GZ, N_GY), (1, N_GZ)]
    for axis_id in range(3):
        stride, count = strides[axis_id]
        source_cell = source_device // stride % count
        owner_cell = owner_device // stride % count
        step = wrapped_step(source_cell, owner_cell, count)
        offset_index = (offset_index * 3 + step + 1).astype(jnp.int32)
        coordinates.append(step.astype(jnp.float32) * TG + flat_parts[axis_id])
    payload = jnp.stack(coordinates + [flat_parts[3], flat_parts[4], flat_parts[5], flat_parts[6]], axis=0)
    member_cells = 27 * GCAP
    position = (safe_label * member_cells + offset_index * GCAP + flat_slots).astype(jnp.int32)
    target = jnp.where(member, position, ngroups * member_cells).astype(jnp.int32)
    buffer = jnp.zeros((7, ngroups * member_cells), jnp.float32)
    buffer = buffer.at[:, target.reshape(-1)].set(payload.reshape(7, -1), mode='drop')
    blocks = jnp.moveaxis(buffer.reshape(7, ngroups // 4, 4, member_cells), 1, 0)
    table = lax.map(group_energy_block, blocks).reshape(ngroups * member_cells)
    picked = table[jnp.where(member, position, 0).astype(jnp.int32)]
    group_energy = jnp.where(member, picked, 0.0).reshape(N_GX, N_GY, N_GZ, slab_all)
    return (edge_potential, group_energy)
```

```python
import functools

import jax
import jax.numpy as jnp
from jax import lax
from jax.experimental import pallas as pl
from jax.experimental.pallas import tpu as pltpu
from jax.sharding import PartitionSpec as P

TG = 8
GCAP = 32
LANES = 128
SOFTENING = 0.01
EDGE_COUPLING = 1.0 / 256.0
GROUP_COUPLING = 1.0 / 16.0
VMEM_LIMIT = 48 * 1024 * 1024
CELL = 40
VMEM = pltpu.VMEM
F32 = jnp.float32
BF16 = jnp.bfloat16
I32 = jnp.int32


def call(kernel, outs, n_in, scratch, smem_first=False):
    specs = [pl.BlockSpec(memory_space=VMEM)] * n_in
    if smem_first:
        specs[0] = pl.BlockSpec(memory_space=pltpu.SMEM)
    return pl.pallas_call(
        kernel,
        out_shape=[jax.ShapeDtypeStruct(s, d) for s, d in outs],
        in_specs=specs,
        out_specs=[pl.BlockSpec(memory_space=VMEM)] * len(outs),
        scratch_shapes=scratch,
        compiler_params=pltpu.CompilerParams(vmem_limit_bytes=VMEM_LIMIT),
    )


def row(ref, index):
    return jnp.broadcast_to(ref[pl.ds(index, 1), :], (8, LANES))


def take_lanes(values, index):
    return jnp.take_along_axis(values, index, axis=1, mode="promise_in_bounds")


STAGES = 9
INVALID = (4096 * 32) << STAGES


def member_kernel(counts, coords, lab_ref, slot_ref, parts_ref, owner_ref,
                  out_m, out_0, out_p, bits_ref, code_ref, vel_ref, blocks_ref,
                  word_ref, buf_ref, lhs_ref, rhs_ref, lhs2_ref, rhs2_ref, acc_ref, acc2_ref):
    rows = lab_ref.shape[0]
    ngroups = owner_ref.shape[0] * LANES
    label = lab_ref[...]
    member = label < ngroups
    flags = jnp.where(member, 1.0, 0.0)
    below = lax.broadcasted_iota(I32, (rows, rows), 0) > lax.broadcasted_iota(I32, (rows, rows), 1)
    rank = jnp.dot(jnp.where(below, 1.0, 0.0).astype(BF16), flags.astype(BF16),
                   preferred_element_type=F32)
    place = lax.broadcasted_iota(I32, (rows, LANES), 0)
    shift = place - rank.astype(I32)
    word = ((label * GCAP + slot_ref[...]) << STAGES) | shift
    word_ref[pl.ds(0, rows), :] = jnp.where(member, word, INVALID)
    word_ref[pl.ds(rows, 256), :] = jnp.full((256, LANES), INVALID, I32)
    bits_ref[...] = jnp.zeros_like(bits_ref)
    for c in range(7):
        buf_ref[c, pl.ds(0, rows), :] = parts_ref[c]
    tops = jnp.max(rank + flags, axis=0, keepdims=True)
    most = jnp.max(tops).astype(I32)
    n_blocks = (most + 7) // 8
    blocks_ref[0] = n_blocks
    step_rows = 32
    for stage in range(STAGES):
        d = 1 << stage

        def move(i, carry, d=d):
            base = pl.multiple_of(i * step_rows, step_rows)
            here = pl.ds(base, step_rows)
            there = pl.ds(base + d, step_rows)
            own = word_ref[here, :]
            far = word_ref[there, :]
            bits_ref[here, :] = bits_ref[here, :] | (own & d)
            comes = (far & d) != 0
            goes = (own & d) != 0
            word_ref[here, :] = jnp.where(comes, far, jnp.where(goes, INVALID, own))
            for c in range(7):
                buf_ref[c, here, :] = jnp.where(comes, buf_ref[c, there, :], buf_ref[c, here, :])
            return carry

        lax.fori_loop(0, rows // step_rows, move, 0)

    acc_ref[...] = jnp.zeros_like(acc_ref)
    acc2_ref[...] = jnp.zeros_like(acc2_ref)
    iota32 = lax.broadcasted_iota(I32, (32, LANES), 0)

    def scatter(i, carry):
        base = pl.multiple_of(i * 8, 8)
        here = pl.ds(base, 8)
        key = word_ref[here, :] >> STAGES
        valid = key < ngroups * GCAP
        lab = key >> 5
        slot = key & 31
        low = lab & 127
        high = lab >> 7
        owner = jnp.zeros((8, LANES), I32)
        for r in range(ngroups // LANES):
            owner = jnp.where(high == r, take_lanes(row(owner_ref, r), low), owner)
        group = owner & 31
        device = owner >> 5
        nx, ny, nz = counts

        def step(mine, theirs, n):
            return ((mine - theirs + (n // 2 + n)) % n) - n // 2 if n & (n - 1) else (
                ((mine - theirs + n // 2) & (n - 1)) - n // 2)

        if all(n & (n - 1) == 0 for n in counts):
            bz, by = nz.bit_length() - 1, ny.bit_length() - 1
            cz, cy, cx = device & (nz - 1), (device >> bz) & (ny - 1), device >> (bz + by)
        else:
            cz, cy, cx = device % nz, device // nz % ny, device // (nz * ny)
        ox = 1 - step(coords[0], cx, nx)
        oy = 1 - step(coords[1], cy, ny)
        oz = 1 - step(coords[2], cz, nz)
        cell = (ox * 3 + oy) * 3 + oz
        cell = jnp.where(valid, cell, -1)
        code = (((ox * 9 + oz * 3 + oy) * 8 + (slot & 7)) << 7) | ((slot >> 3) << 5) | group
        code_ref[here, :] = jnp.where(valid, code, 0)
        mass = buf_ref[6, here, :]
        vals = [buf_ref[0, here, :] - 0.5 * TG, buf_ref[1, here, :] - 0.5 * TG,
                buf_ref[2, here, :] - 0.5 * TG, mass]
        moms = []
        for c in range(3):
            v = buf_ref[3 + c, here, :]
            vel_ref[c, here, :] = v
            moms.append(mass * v)
        high_part = [v.astype(BF16).astype(F32) for v in vals + moms]
        low_part = [v - h for v, h in zip(vals + moms, high_part)]
        for r in range(8):
            lanes = slice(r * LANES, (r + 1) * LANES)
            group_r = jnp.broadcast_to(group[r:r + 1], (32, LANES))
            slot_r = jnp.broadcast_to(slot[r:r + 1], (32, LANES))
            cell_r = jnp.broadcast_to(cell[r:r + 1], (32, LANES))
            at_group = iota32 == group_r
            at_slot = iota32 == slot_r
            hot = jnp.where(at_group, 1.0, 0.0)
            for d in range(27):
                lhs_ref[d * 32:(d + 1) * 32, lanes] = jnp.where(cell_r == d, hot, 0.0).astype(BF16)
            lhs2_ref[:, lanes] = jnp.where(iota32 == cell_r, 1.0, 0.0).astype(BF16)
            for half, parts in ((0, high_part), (1, low_part)):
                for c in range(4):
                    v = jnp.broadcast_to(parts[c][r:r + 1], (32, LANES))
                    o = half * 128 + c * 32
                    rhs_ref[o:o + 32, lanes] = jnp.where(at_slot, v, 0.0).astype(BF16)
                for c in range(3):
                    v = jnp.broadcast_to(parts[4 + c][r:r + 1], (32, LANES))
                    o = half * 128 + c * 32
                    rhs2_ref[o:o + 32, lanes] = jnp.where(at_group, v, 0.0).astype(BF16)
        nt = (((1,), (1,)), ((), ()))
        acc_ref[...] += lax.dot_general(lhs_ref[...], rhs_ref[...], nt, preferred_element_type=F32)
        acc2_ref[...] += lax.dot_general(lhs2_ref[...], rhs2_ref[...], nt, preferred_element_type=F32)
        return carry

    rhs2_ref[...] = jnp.zeros_like(rhs2_ref)
    lax.fori_loop(0, n_blocks, scatter, 0)
    tiles = TG * TG
    for a, out in enumerate((out_m, out_0, out_p)):
        for e in range(9):
            d = a * 9 + e
            out[e * CELL:e * CELL + 32, :] = (acc_ref[d * 32:(d + 1) * 32, 0:128]
                                              + acc_ref[d * 32:(d + 1) * 32, 128:256])
            mom = acc2_ref[d:d + 1, 0:128] + acc2_ref[d:d + 1, 128:256]
            out[e * CELL + 32:e * CELL + 40, :] = jnp.broadcast_to(mom, (8, LANES))
    for out, face in ((out_m, 0), (out_p, 1)):
        for k, c in enumerate((0, 1, 2, 6)):
            out[9 * CELL + k * tiles:9 * CELL + (k + 1) * tiles, :] = (
                parts_ref[c, face * tiles:(face + 1) * tiles, :])


def members(coords, counts, labels, slots, parts, owner):
    rows = labels.shape[0]
    send = (9 * CELL + 4 * TG * TG, LANES)

    def kernel(coords_ref, lab, slot, parts_r, own, *rest):
        outs, scratch = rest[:7], rest[7:]
        member_kernel(counts, [coords_ref[k] for k in range(3)], lab, slot, parts_r, own, *outs, *scratch)

    specs = [pl.BlockSpec(memory_space=VMEM)] * 7
    specs[6] = pl.BlockSpec(memory_space=pltpu.SMEM)
    shapes = [(send, F32), ((9 * CELL, LANES), F32), (send, F32), ((rows, LANES), I32),
              ((rows, LANES), I32), ((3, rows, LANES), F32), ((1,), I32)]
    return pl.pallas_call(
        kernel,
        out_shape=[jax.ShapeDtypeStruct(s, d) for s, d in shapes],
        in_specs=[pl.BlockSpec(memory_space=pltpu.SMEM)] + [pl.BlockSpec(memory_space=VMEM)] * 4,
        out_specs=specs,
        scratch_shapes=[
            VMEM((rows + 256, LANES), I32),
            VMEM((7, rows + 256, LANES), F32),
            VMEM((27 * 32, 1024), BF16),
            VMEM((256, 1024), BF16),
            VMEM((32, 1024), BF16),
            VMEM((256, 1024), BF16),
            VMEM((27 * 32, 256), F32),
            VMEM((32, 256), F32),
        ],
        compiler_params=pltpu.CompilerParams(vmem_limit_bytes=VMEM_LIMIT),
    )(coords, labels, slots, parts, owner)


def inverse_distance(target, source):
    dx = target[0] - source[0]
    dy = target[1] - source[1]
    dz = target[2] - source[2]
    return lax.rsqrt(dx * dx + dy * dy + (dz * dz + SOFTENING))


def sym_pairs(target, acc, source, base, first, offsets, once=(), skip_self=False, lone=()):
    src = [[row(ref, base + first + r) for ref in source] for r in range(4)]
    gains = [jnp.zeros((8, LANES), F32) for _ in range(4)]
    sublane = lax.broadcasted_iota(I32, (8, LANES), 0)
    for t in list(offsets) + list(lone):
        at = pl.ds(pl.multiple_of(base + 8 * t, 8), 8)
        tgt = [ref[at, :] for ref in target]
        total = acc[at, :]
        for r in range(4):
            inv = inverse_distance(tgt, src[r])
            mine = inv * src[r][3]
            if skip_self and t == 0:
                mine = jnp.where(sublane == first + r, 0.0, mine)
            total = total + mine
            if t in offsets:
                gains[r] = gains[r] + inv * tgt[3]
        acc[at, :] = total
    return [jnp.sum(g, axis=0, keepdims=True) for g in gains]


def near_kernel(parts_ref, out_ref, xs, ys, zs, ms, acc):
    target = (xs, ys, zs, ms)
    tiles = 2 * TG * TG
    for axis in range(3):
        for ref, c in zip(target, (0, 1, 2, 6)):
            t = jnp.transpose(parts_ref[c, axis * tiles:(axis + 1) * tiles, :])
            ref[0:128, :] = t
            ref[128:256, :] = t
        acc[...] = jnp.zeros_like(acc)

        def body(jb, carry):
            base = pl.multiple_of(jb * 8, 8)
            for first in (0, 4):
                gains = sym_pairs(target, acc, target, base, first, range(1, 8), skip_self=True, lone=(0, 8))
                for r in range(4):
                    at = pl.ds(base + first + r, 1)
                    acc[at, :] = acc[at, :] + gains[r]
            return carry

        lax.fori_loop(0, 16, body, 0)
        out_ref[axis * 128:(axis + 1) * 128, :] = acc[0:128, :] + acc[128:256, :]


def far_kernel(axis, parts_ref, near_ref, low_ref, high_ref, out_ref, xs, ys, zs, ms, acc):
    tiles = TG * TG
    source = (xs, ys, zs, ms)
    target = []
    for k, (ref, c) in enumerate(zip(source, (0, 1, 2, 6))):
        low = low_ref[k * tiles:(k + 1) * tiles, :]
        high = high_ref[k * tiles:(k + 1) * tiles, :]
        if k == axis:
            low = low - 1.0 * TG
            high = high + 1.0 * TG
        ref[...] = jnp.transpose(jnp.concatenate([low, high], axis=0))
    tgt_refs = acc
    for k, c in enumerate((0, 1, 2)):
        tgt_refs[k, :, :] = jnp.transpose(parts_ref[c, axis * 2 * tiles:(axis + 1) * 2 * tiles, :])
    tgt_refs[3, :, :] = near_ref[axis * 128:(axis + 1) * 128, :]

    def body(jb, carry):
        base = pl.multiple_of(jb * 4, 4)
        src = [[row(ref, base + r) for ref in source] for r in range(4)]
        for t in range(16):
            at = slice(8 * t, 8 * t + 8)
            tgt = [tgt_refs[k, at, :] for k in range(3)]
            total = tgt_refs[3, at, :]
            for r in range(4):
                total = total + inverse_distance(tgt, src[r]) * src[r][3]
            tgt_refs[3, at, :] = total
        return carry

    lax.fori_loop(0, 32, body, 0)
    out_ref[...] = jnp.transpose(tgt_refs[3, :, :]) * (-EDGE_COUPLING)


def near(parts):
    return call(near_kernel, [((384, LANES), F32)], 1, [VMEM((256, LANES), F32)] * 5)(parts)[0]


def far(axis, parts, near_part, low, high):
    return call(functools.partial(far_kernel, axis), [((128, LANES), F32)], 4,
                [VMEM((128, LANES), F32)] * 4 + [VMEM((4, 128, LANES), F32)])(
                    parts, near_part, low, high)[0]


def group_kernel(low_ref, mid_ref, high_ref, out_m, out_0, out_p,
                 x0, y0, z0, m0, acc, s1, s2, g1, g2):
    base = (x0, y0, z0, m0)
    n_rows = 27 * 8
    quarter = lax.broadcasted_iota(I32, (8, LANES), 1) // 32
    received = (low_ref, mid_ref, high_ref)
    mom = jnp.zeros((8, LANES), F32)
    cells = []
    for e in range(28):
        if e == 27:
            cells.append(jnp.zeros((32, LANES), F32))
        else:
            ref, within = received[e // 9], e % 9
            cells.append(ref[within * CELL:within * CELL + 32, :])
            mom = mom + ref[within * CELL + 32:within * CELL + 40, :]
    for blk in range(7):
        flat = jnp.transpose(jnp.concatenate(cells[blk * 4:blk * 4 + 4], axis=0))
        for c in range(4):
            quads = [flat[c * 32 + q * 8:c * 32 + q * 8 + 8, :] for q in range(4)]
            for a in range(4):
                e = blk * 4 + a
                if e == 27:
                    continue
                mixed = None
                for q in range(4):
                    moved = quads[q] if q == a else pltpu.roll(quads[q], (32 * (q - a)) % 128, 1)
                    mixed = moved if mixed is None else jnp.where(quarter == q, moved, mixed)
                if c < 3:
                    d = (e % 3, e // 3 % 3, e // 9)[c] - 1
                    mixed = mixed + float(TG * d)
                base[c][e * 8:e * 8 + 8, :] = mixed
                base[c][n_rows + e * 8:n_rows + e * 8 + 8, :] = mixed
    for c in range(4):
        v = base[c][0:n_rows, :]
        s1[c, :, :] = pltpu.roll(v, 96, 1)
        s2[c, :, :] = pltpu.roll(v, 64, 1)
    acc[...] = jnp.zeros_like(acc)
    src1 = tuple(s1.at[c] for c in range(4))
    src2 = tuple(s2.at[c] for c in range(4))

    def body(jb, carry):
        at0 = pl.multiple_of(jb * 8, 8)
        for first in (0, 4):
            own = sym_pairs(base, acc, base, at0, first, range(1, 14), skip_self=True, lone=(0,))
            one = sym_pairs(base, acc, src1, at0, first, range(0, 27))
            two = sym_pairs(base, acc, src2, at0, first, range(1, 14), lone=(0,))
            for r in range(4):
                at = pl.ds(at0 + first + r, 1)
                acc[at, :] = acc[at, :] + own[r]
                g1[at, :] = one[r]
                g2[at, :] = two[r]
        return carry

    lax.fori_loop(0, 27, body, 0)
    total = (acc[0:n_rows, :] + acc[n_rows:2 * n_rows, :]
             + pltpu.roll(g1[...], 32, 1) + pltpu.roll(g2[...], 64, 1))
    mass = jnp.sum(m0[0:n_rows, :], axis=0, keepdims=True)
    mass = jnp.broadcast_to(mass, (8, LANES))
    mass = mass + pltpu.roll(mass, 32, 1)
    mass = mass + pltpu.roll(mass, 64, 1)
    mean = mom / mass
    for zs, out in enumerate((out_m, out_0, out_p)):
        out[0:72, :] = total[zs * 72:(zs + 1) * 72, :] * (-GROUP_COUPLING)
        out[72:80, :] = mean


def groups(low, mid, high):
    rows = 27 * 8
    return call(group_kernel, [((80, LANES), F32)] * 3, 3,
                [VMEM((2 * rows, LANES), F32)] * 5 + [VMEM((4, rows, LANES), F32)] * 2
                + [VMEM((rows, LANES), F32)] * 2)(low, mid, high)


def energy_kernel(blocks_ref, low_ref, mid_ref, high_ref, code_ref, vel_ref, bits_ref, lab_ref, out_ref, buf_ref):
    received = (low_ref, mid_ref, high_ref)
    rows = code_ref.shape[0]

    def gather(i, carry):
        base = pl.multiple_of(i * 8, 8)
        here = pl.ds(base, 8)
        code = code_ref[here, :]
        lane = code & 127
        at_row = code >> 7
        at_cell = code >> 10
        group = code & 31
        lanes = [group + 32 * c for c in range(3)]
        pot = jnp.zeros((8, LANES), F32)
        mean = [jnp.zeros((8, LANES), F32) for _ in range(3)]
        for cell in range(27):
            ref, within = received[cell // 9], cell % 9
            for s in range(8):
                got = take_lanes(row(ref, within * 16 + s), lane)
                pot = jnp.where(at_row == cell * 8 + s, got, pot)
            src = row(ref, within * 16 + 8)
            for c in range(3):
                mean[c] = jnp.where(at_cell == cell, take_lanes(src, lanes[c]), mean[c])
        kinetic = jnp.zeros((8, LANES), F32)
        for c in range(3):
            diff = vel_ref[c, here, :] - mean[c]
            kinetic = kinetic + diff * diff
        buf_ref[pl.ds(pl.multiple_of(base + 256, 8), 8), :] = pot + 0.5 * kinetic
        return carry

    lax.fori_loop(0, blocks_ref[0], gather, 0)
    step_rows = 32
    for stage in reversed(range(STAGES)):
        d = 1 << stage

        def move(i, carry, d=d):
            base = pl.multiple_of((rows // step_rows - 1 - i) * step_rows, step_rows)
            moved = (bits_ref[pl.ds(base, step_rows), :] & d) != 0
            here = pl.ds(pl.multiple_of(base + 256, 8), step_rows)
            buf_ref[here, :] = jnp.where(moved, buf_ref[pl.ds(base + 256 - d, step_rows), :], buf_ref[here, :])
            return carry

        lax.fori_loop(0, rows // step_rows, move, 0)
    out_ref[...] = jnp.where(lab_ref[...] < 4096, buf_ref[pl.ds(256, rows), :], 0.0)


def energies(blocks, low, mid, high, code, vel, bits, labels):
    rows = labels.shape[0]
    return call(energy_kernel, [((rows, LANES), F32)], 8, [VMEM((rows + 256, LANES), F32)], smem_first=True)(
        blocks, low, mid, high, code, vel, bits, labels)[0]


def up(axis, x):
    n = lax.axis_size(axis)
    return lax.ppermute(x, axis, [(i, (i + 1) % n) for i in range(n)])


def down(axis, x):
    n = lax.axis_size(axis)
    return lax.ppermute(x, axis, [((i + 1) % n, i) for i in range(n)])


def local(particles, labels, member_slot, owner_slot):
    slab_all = particles.shape[-1]
    rows = slab_all // LANES
    parts = particles.reshape(7, rows, LANES)
    lab = labels.reshape(rows, LANES)
    slots = member_slot.reshape(rows, LANES)
    owner = owner_slot.reshape(-1, LANES)
    counts = tuple(lax.axis_size(a) for a in ("gx", "gy", "gz"))
    coords = jnp.stack([lax.axis_index(a) for a in ("gx", "gy", "gz")]).astype(I32)
    tiles = TG * TG
    top = 9 * CELL

    def face(k):
        return [parts[c, k * tiles:(k + 1) * tiles] for c in (0, 1, 2, 6)]

    send_m, keep, send_p, bits, code, vel, n_blocks = members(coords, counts, lab, slots, parts, owner)
    from_low = up("gx", send_p)
    from_high = down("gx", send_m)
    near_part = near(parts)
    edge_x = far(0, parts, near_part, from_low[top:], from_high[top:])
    third = 3 * CELL

    def stack_y(b):
        return [t[b * third:(b + 1) * third] for t in (from_low, keep, from_high)]

    y_low = up("gy", jnp.concatenate(stack_y(2) + face(3), axis=0))
    y_high = down("gy", jnp.concatenate(stack_y(0) + face(2), axis=0))
    y_keep = jnp.concatenate(stack_y(1), axis=0)
    edge_y = far(1, parts, near_part, y_low[top:], y_high[top:])

    def stack_z(b):
        return [t[(3 * xs + b) * CELL:(3 * xs + b + 1) * CELL] for t in (y_low, y_keep, y_high) for xs in range(3)]

    z_low = up("gz", jnp.concatenate(stack_z(2) + face(5), axis=0))
    z_high = down("gz", jnp.concatenate(stack_z(0) + face(4), axis=0))
    z_keep = jnp.concatenate(stack_z(1), axis=0)
    edge_z = far(2, parts, near_part, z_low[top:], z_high[top:])
    to_low, stay, to_high = groups(z_low[:top], z_keep, z_high[:top])
    back_high = down("gz", to_low)
    back_low = up("gz", to_high)
    zs = (back_low, stay, back_high)

    def back_y(b):
        return jnp.concatenate([p for t in zs for p in (t[b * 24:(b + 1) * 24], t[72:80])], axis=0)

    ylow = up("gy", back_y(2))
    yhigh = down("gy", back_y(0))
    ys = (ylow, back_y(1), yhigh)

    def back_x(b):
        return jnp.concatenate(
            [p for z in range(3) for t in ys
             for p in (t[z * 32 + b * 8:z * 32 + b * 8 + 8], t[z * 32 + 24:z * 32 + 32])], axis=0)

    xlow = up("gx", back_x(2))
    xhigh = down("gx", back_x(0))
    energy = energies(n_blocks, xlow, back_x(1), xhigh, code, vel, bits, lab)
    edge = jnp.concatenate([edge_x, edge_y, edge_z], axis=0)
    return edge.reshape(1, 1, 1, slab_all), energy.reshape(1, 1, 1, slab_all)


def solution(mesh):
    return jax.shard_map(
        local,
        mesh=mesh,
        in_specs=(
            P(None, "gx", "gy", "gz", None),
            P("gx", "gy", "gz", None),
            P("gx", "gy", "gz", None),
            P(),
        ),
        out_specs=(P("gx", "gy", "gz", None), P("gx", "gy", "gz", None)),
        check_vma=False,
    )
```

```python
import functools

import jax
import jax.numpy as jnp
from jax import lax
from jax.experimental import pallas as pl
from jax.experimental.pallas import tpu as pltpu
from jax.sharding import PartitionSpec as P

TG = 8
GCAP = 32
LANES = 128
SOFTENING = 0.01
EDGE_COUPLING = 1.0 / 256.0
GROUP_COUPLING = 1.0 / 16.0
VMEM_LIMIT = 32 * 1024 * 1024
MEMBER_ROWS = 9 * 32
TOP = MEMBER_ROWS + 8
TOP_X = MEMBER_ROWS + 24
VMEM = pltpu.VMEM
F32 = jnp.float32
BF16 = jnp.bfloat16
I32 = jnp.int32


def call(kernel, outs, n_in, scratch, smem_first=False, after=()):
    after = tuple(a[0:8] for a in after)
    specs = [pl.BlockSpec(memory_space=VMEM)] * n_in + [pl.BlockSpec(memory_space=VMEM)] * len(after)
    if smem_first:
        specs[0] = pl.BlockSpec(memory_space=pltpu.SMEM)

    def body(*refs):
        kernel(*refs[:n_in], *refs[n_in + len(after):])

    run = pl.pallas_call(
        body,
        out_shape=[jax.ShapeDtypeStruct(s, d) for s, d in outs],
        in_specs=specs,
        out_specs=[pl.BlockSpec(memory_space=VMEM)] * len(outs),
        scratch_shapes=scratch,
        compiler_params=pltpu.CompilerParams(vmem_limit_bytes=VMEM_LIMIT),
    )
    return lambda *args: run(*args, *after)


def row(ref, index):
    return jnp.broadcast_to(ref[pl.ds(index, 1), :], (8, LANES))


def take_lanes(values, index):
    return jnp.take_along_axis(values, index, axis=1, mode="promise_in_bounds")


STAGES = 9
INVALID = (4096 * 32) << STAGES
PAD = 16
NT = (((1,), (1,)), ((), ()))


def owner_offset(mine, theirs, n):
    if n & (n - 1):
        step = (mine - theirs + n // 2 + n) % n - n // 2
    else:
        step = ((mine - theirs + n // 2) & (n - 1)) - n // 2
    return 1 - step


def member_kernel(counts, coords, table_hbm, parts_hbm,
                  out_m, out_0, out_p, faces_ref, bits_ref, code_ref, vel_ref, blocks_ref,
                  word_ref, buf_ref, table_ref, cell_ref, lhs_a, lhs_b, rhs_a, rhs_b,
                  lhs2_a, lhs2_b, rhs2_a, rhs2_b, acc_ref, acc2_ref, sems):
    rows = parts_hbm.shape[1]
    owner_ref = table_ref.at[pl.ds(rows, table_ref.shape[0] - rows), :]
    ngroups = owner_ref.shape[0] * LANES
    copies = [
        pltpu.make_async_copy(table_hbm, table_ref, sems.at[0]),
        pltpu.make_async_copy(parts_hbm, buf_ref.at[:, pl.ds(0, rows), :], sems.at[1]),
    ]
    for copy in copies:
        copy.start()
    word_ref[pl.ds(rows, 256), :] = jnp.full((256, LANES), INVALID, I32)
    acc_ref[...] = jnp.zeros_like(acc_ref)
    acc2_ref[...] = jnp.zeros_like(acc2_ref)
    bits_ref[...] = jnp.zeros_like(bits_ref)
    for c in range(7):
        buf_ref[c, pl.ds(rows, PAD), :] = jnp.zeros((PAD, LANES), F32)
    below = lax.broadcasted_iota(I32, (rows, rows), 0) > lax.broadcasted_iota(I32, (rows, rows), 1)
    below = jnp.where(below, 1.0, 0.0).astype(BF16)
    copies[0].wait()
    keys = table_ref[0:rows, :]
    member = keys < ngroups * GCAP
    flags = jnp.where(member, 1.0, 0.0)
    rank = jnp.dot(below, flags.astype(BF16), preferred_element_type=F32)
    place = lax.broadcasted_iota(I32, (rows, LANES), 0)
    shift = place - rank.astype(I32)
    word = (keys << STAGES) | shift
    word_ref[pl.ds(0, rows), :] = jnp.where(member, word, INVALID)
    tops = jnp.max(rank + flags, axis=0, keepdims=True)
    n_blocks = (jnp.max(tops).astype(I32) + 7) // 8
    blocks_ref[0] = n_blocks
    copies[1].wait()
    tiles = TG * TG
    for out, face in ((out_m, 0), (out_p, 1)):
        for k, c in enumerate((0, 1, 2, 6)):
            out[TOP_X + k * tiles:TOP_X + (k + 1) * tiles, :] = buf_ref[c, face * tiles:(face + 1) * tiles, :]
    for face in range(2, 6):
        for k, c in enumerate((0, 1, 2, 6)):
            faces_ref[face - 2, k * tiles:(k + 1) * tiles, :] = buf_ref[c, face * tiles:(face + 1) * tiles, :]
    step_rows = 32
    for stage in range(STAGES):
        d = 1 << stage

        def move(i, carry, d=d):
            base = pl.multiple_of(i * step_rows, step_rows)
            here = pl.ds(base, step_rows)
            there = pl.ds(base + d, step_rows)
            own = word_ref[here, :]
            far = word_ref[there, :]
            bits_ref[here, :] = bits_ref[here, :] | (own & d)
            comes = (far & d) != 0
            goes = (own & d) != 0
            word_ref[here, :] = jnp.where(comes, far, jnp.where(goes, INVALID, own))
            for c in range(7):
                buf_ref[c, here, :] = jnp.where(comes, buf_ref[c, there, :], buf_ref[c, here, :])
            return carry

        lax.fori_loop(0, rows // step_rows, move, 0)

    iota32 = lax.broadcasted_iota(I32, (32, LANES), 0)
    iota_b = iota32.astype(F32).astype(BF16)
    zero_b = jnp.zeros((32, LANES), BF16)
    one_b = jnp.ones((32, LANES), BF16)

    def decode(i, carry):
        here = pl.ds(pl.multiple_of(i * PAD, PAD), PAD)
        key = word_ref[here, :] >> STAGES
        valid = key < ngroups * GCAP
        lab = key >> 5
        slot = key & 31
        low = lab & 127
        high = lab >> 7
        owner = jnp.zeros((PAD, LANES), I32)
        for r in range(ngroups // LANES):
            found = take_lanes(jnp.broadcast_to(owner_ref[pl.ds(r, 1), :], (PAD, LANES)), low)
            owner = jnp.where(high == r, found, owner)
        group = owner & 31
        device = owner >> 5
        nx, ny, nz = counts
        ox = owner_offset(coords[0], device // (nz * ny), nx)
        oy = owner_offset(coords[1], device // nz % ny, ny)
        oz = owner_offset(coords[2], device % nz, nz)
        cell_ref[here, :] = jnp.where(valid, (ox * 3 + oy) * 3 + oz, -1).astype(F32)
        code = (((ox * 9 + oz * 3 + oy) * 8 + (slot & 7)) << 7) | ((slot >> 3) << 5) | group
        code_ref[here, :] = jnp.where(valid, code, 0)
        return carry

    lax.fori_loop(0, jnp.minimum((n_blocks + 4) // 2, (rows + PAD) // PAD), decode, 0)

    def build(i, lhs, rhs, lhs2, rhs2):
        here = pl.ds(pl.multiple_of(i * 8, 8), 8)
        cell = cell_ref[here, :]
        code = code_ref[here, :]
        slot = (((code >> 5) & 3) << 3) | ((code >> 7) & 7)
        group = code & 31
        mass = buf_ref[6, here, :]
        vals = [buf_ref[c, here, :] - 0.5 * TG for c in range(3)] + [mass]
        for c in range(3):
            v = buf_ref[3 + c, here, :]
            vel_ref[c, here, :] = v
            vals.append(mass * v)
        high_part = [v.astype(BF16).astype(F32) for v in vals]
        low_part = [v - h for v, h in zip(vals, high_part)]
        slot_f, group_f = slot.astype(F32), group.astype(F32)

        def spread(v, r):
            return jnp.broadcast_to(v[r:r + 1], (32, LANES)).astype(BF16)

        for r in range(8):
            lanes = slice(r * LANES, (r + 1) * LANES)
            at_group = iota_b == spread(group_f, r)
            at_slot = iota_b == spread(slot_f, r)
            cell_r = spread(cell, r)
            hot = jnp.where(at_group, one_b, zero_b)
            for d in range(27):
                lhs[d * 32:(d + 1) * 32, lanes] = jnp.where(cell_r == jnp.asarray(d, BF16), hot, zero_b)
            lhs2[:, lanes] = jnp.where(iota_b == cell_r, one_b, zero_b)
            for half, parts in ((0, high_part), (1, low_part)):
                for c in range(4):
                    o = half * 128 + c * 32
                    rhs[o:o + 32, lanes] = jnp.where(at_slot, spread(parts[c], r), zero_b)
                for c in range(3):
                    o = half * 96 + c * 32
                    rhs2[o:o + 32, lanes] = jnp.where(at_group, spread(parts[4 + c], r), zero_b)

    def add(lhs, rhs, lhs2, rhs2):
        acc_ref[...] += lax.dot_general(lhs[...], rhs[...], NT, preferred_element_type=F32)
        acc2_ref[0:32, :] += lax.dot_general(lhs2[...], rhs2[...], NT, preferred_element_type=F32)

    slot_a = (lhs_a, rhs_a, lhs2_a, rhs2_a)
    slot_b = (lhs_b, rhs_b, lhs2_b, rhs2_b)
    build(0, *slot_a)

    def scatter(i, carry):
        build(2 * i + 1, *slot_b)
        add(*slot_a)
        build(2 * i + 2, *slot_a)
        add(*slot_b)
        return carry

    lax.fori_loop(0, (n_blocks + 1) // 2, scatter, 0)
    for a, out in enumerate((out_m, out_0, out_p)):
        out[0:288, :] = acc_ref[a * 288:(a + 1) * 288, 0:128] + acc_ref[a * 288:(a + 1) * 288, 128:256]
        for b in range(3):
            at = slice(MEMBER_ROWS + 8 * b, MEMBER_ROWS + 8 * b + 8)
            first = a * 9 + b * 3
            mom = acc2_ref[first:first + 8, 0:96] + acc2_ref[first:first + 8, 96:192]
            out[at, :] = jnp.concatenate([mom, jnp.zeros((8, 32), F32)], axis=1)


def members(coords, counts, table, parts):
    rows = parts.shape[1]
    send = (TOP_X + 4 * TG * TG, LANES)

    def kernel(coords_ref, *rest):
        member_kernel(counts, [coords_ref[k] for k in range(3)], *rest)

    shapes = [(send, F32), ((TOP_X, LANES), F32), (send, F32), ((4, 4 * TG * TG, LANES), F32), ((rows, LANES), I32),
              ((rows + PAD, LANES), I32), ((3, rows + PAD, LANES), F32), ((1,), I32)]
    specs = [pl.BlockSpec(memory_space=VMEM)] * 8
    specs[7] = pl.BlockSpec(memory_space=pltpu.SMEM)
    return pl.pallas_call(
        kernel,
        out_shape=[jax.ShapeDtypeStruct(s, d) for s, d in shapes],
        in_specs=[pl.BlockSpec(memory_space=m) for m in [pltpu.SMEM] + [pltpu.HBM] * 2],
        out_specs=specs,
        scratch_shapes=[
            VMEM((rows + 256, LANES), I32),
            VMEM((7, rows + 256, LANES), F32),
            VMEM(table.shape, I32),
            VMEM((rows + PAD, LANES), F32),
        ] + [VMEM((27 * 32, 1024), BF16)] * 2 + [VMEM((256, 1024), BF16)] * 2
        + [VMEM((32, 1024), BF16)] * 2 + [VMEM((192, 1024), BF16)] * 2 + [
            VMEM((27 * 32, 256), F32),
            VMEM((40, 192), F32),
            pltpu.SemaphoreType.DMA((2,)),
        ],
        compiler_params=pltpu.CompilerParams(vmem_limit_bytes=VMEM_LIMIT),
    )(coords, table, parts)


def inverse_distance(target, source):
    dx = target[0] - source[0]
    dy = target[1] - source[1]
    dz = target[2] - source[2]
    return lax.rsqrt(dx * dx + dy * dy + (dz * dz + SOFTENING))


def sym_pairs(target, acc, source, base, first, offsets, once=(), skip_self=False, lone=()):
    src = [[row(ref, base + first + r) for ref in source] for r in range(4)]
    gains = [jnp.zeros((8, LANES), F32) for _ in range(4)]
    sublane = lax.broadcasted_iota(I32, (8, LANES), 0)
    for t in list(offsets) + list(lone):
        at = pl.ds(pl.multiple_of(base + 8 * t, 8), 8)
        tgt = [ref[at, :] for ref in target]
        total = acc[at, :]
        for r in range(4):
            inv = inverse_distance(tgt, src[r])
            mine = inv * src[r][3]
            if skip_self and t == 0:
                mine = jnp.where(sublane == first + r, 0.0, mine)
            total = total + mine
            if t in offsets:
                gains[r] = gains[r] + inv * tgt[3]
        acc[at, :] = total
    return [jnp.sum(g, axis=0, keepdims=True) for g in gains]


def near_kernel(axes, parts_ref, out_ref, xs, ys, zs, ms, acc):
    target = (xs, ys, zs, ms)
    tiles = 2 * TG * TG
    for k, axis in enumerate(axes):
        for ref, c in zip(target, (0, 1, 2, 6)):
            t = jnp.transpose(parts_ref[c, axis * tiles:(axis + 1) * tiles, :])
            ref[0:128, :] = t
            ref[128:256, :] = t
        acc[...] = jnp.zeros_like(acc)

        def body(jb, carry):
            base = pl.multiple_of(jb * 8, 8)
            for first in (0, 4):
                gains = sym_pairs(target, acc, target, base, first, range(1, 8), skip_self=True, lone=(0, 8))
                for r in range(4):
                    at = pl.ds(base + first + r, 1)
                    acc[at, :] = acc[at, :] + gains[r]
            return carry

        lax.fori_loop(0, 16, body, 0)
        out_ref[k * 128:(k + 1) * 128, :] = acc[0:128, :] + acc[128:256, :]


def far_kernel(axis, parts_ref, near_ref, low_ref, high_ref, out_ref, xs, ys, zs, ms, acc):
    tiles = TG * TG
    source = (xs, ys, zs, ms)
    target = []
    for k, (ref, c) in enumerate(zip(source, (0, 1, 2, 6))):
        low = low_ref[k * tiles:(k + 1) * tiles, :]
        high = high_ref[k * tiles:(k + 1) * tiles, :]
        if k == axis:
            low = low - 1.0 * TG
            high = high + 1.0 * TG
        ref[...] = jnp.transpose(jnp.concatenate([low, high], axis=0))
    tgt_refs = acc
    for k, c in enumerate((0, 1, 2)):
        tgt_refs[k, :, :] = jnp.transpose(parts_ref[c, axis * 2 * tiles:(axis + 1) * 2 * tiles, :])
    tgt_refs[3, :, :] = near_ref[...]

    def body(jb, carry):
        base = pl.multiple_of(jb * 4, 4)
        src = [[row(ref, base + r) for ref in source] for r in range(4)]
        for t in range(16):
            at = slice(8 * t, 8 * t + 8)
            tgt = [tgt_refs[k, at, :] for k in range(3)]
            total = tgt_refs[3, at, :]
            for r in range(4):
                total = total + inverse_distance(tgt, src[r]) * src[r][3]
            tgt_refs[3, at, :] = total
        return carry

    lax.fori_loop(0, 32, body, 0)
    out_ref[...] = jnp.transpose(tgt_refs[3, :, :]) * (-EDGE_COUPLING)


def near(axes, parts, after):
    return call(functools.partial(near_kernel, axes), [((128 * len(axes), LANES), F32)], 1,
                [VMEM((256, LANES), F32)] * 5, after=after)(parts)[0]


def far(axis, parts, near_part, low, high, after=()):
    return call(functools.partial(far_kernel, axis), [((128, LANES), F32)], 4,
                [VMEM((128, LANES), F32)] * 4 + [VMEM((4, 128, LANES), F32)], after=after)(
                    parts, near_part, low, high)[0]


def group_kernel(low_ref, mid_ref, high_ref, out_m, out_0, out_p,
                 x0, y0, z0, m0, acc, s1, s2, g1, g2):
    base = (x0, y0, z0, m0)
    n_rows = 27 * 8
    quarter = lax.broadcasted_iota(I32, (8, LANES), 1) // 32
    received = (low_ref, mid_ref, high_ref)
    mom = jnp.zeros((8, LANES), F32)
    cells = []
    for e in range(28):
        if e == 27:
            cells.append(jnp.zeros((32, LANES), F32))
        else:
            ref, within = received[e // 9], e % 9
            cells.append(ref[within * 32:within * 32 + 32, :])
    for ref, dz in zip(received, (2, 1, 0)):
        mom = mom + jnp.broadcast_to(ref[MEMBER_ROWS + dz:MEMBER_ROWS + dz + 1, :], (8, LANES))
    for blk in range(7):
        flat = jnp.transpose(jnp.concatenate(cells[blk * 4:blk * 4 + 4], axis=0))
        for c in range(4):
            quads = [flat[c * 32 + q * 8:c * 32 + q * 8 + 8, :] for q in range(4)]
            for a in range(4):
                e = blk * 4 + a
                if e == 27:
                    continue
                mixed = None
                for q in range(4):
                    moved = quads[q] if q == a else pltpu.roll(quads[q], (32 * (q - a)) % 128, 1)
                    mixed = moved if mixed is None else jnp.where(quarter == q, moved, mixed)
                if c < 3:
                    d = (e % 3, e // 3 % 3, e // 9)[c] - 1
                    mixed = mixed + float(TG * d)
                base[c][e * 8:e * 8 + 8, :] = mixed
                base[c][n_rows + e * 8:n_rows + e * 8 + 8, :] = mixed
    for c in range(4):
        v = base[c][0:n_rows, :]
        s1[c, :, :] = pltpu.roll(v, 96, 1)
        s2[c, :, :] = pltpu.roll(v, 64, 1)
    acc[...] = jnp.zeros_like(acc)
    src1 = tuple(s1.at[c] for c in range(4))
    src2 = tuple(s2.at[c] for c in range(4))

    def body(jb, carry):
        at0 = pl.multiple_of(jb * 8, 8)
        for first in (0, 4):
            own = sym_pairs(base, acc, base, at0, first, range(1, 14), skip_self=True, lone=(0,))
            one = sym_pairs(base, acc, src1, at0, first, range(0, 27))
            two = sym_pairs(base, acc, src2, at0, first, range(1, 14), lone=(0,))
            for r in range(4):
                at = pl.ds(at0 + first + r, 1)
                acc[at, :] = acc[at, :] + own[r]
                g1[at, :] = one[r]
                g2[at, :] = two[r]
        return carry

    lax.fori_loop(0, 27, body, 0)
    total = (acc[0:n_rows, :] + acc[n_rows:2 * n_rows, :]
             + pltpu.roll(g1[...], 32, 1) + pltpu.roll(g2[...], 64, 1))
    mass = jnp.sum(m0[0:n_rows, :], axis=0, keepdims=True)
    mass = jnp.broadcast_to(mass, (8, LANES))
    mass = mass + pltpu.roll(mass, 32, 1)
    mass = mass + pltpu.roll(mass, 64, 1)
    mean = mom / mass
    for zs, out in enumerate((out_m, out_0, out_p)):
        out[0:72, :] = total[zs * 72:(zs + 1) * 72, :] * (-GROUP_COUPLING)
        out[72:80, :] = mean


def groups(low, mid, high, after):
    rows = 27 * 8
    return call(group_kernel, [((80, LANES), F32)] * 3, 3,
                [VMEM((2 * rows, LANES), F32)] * 5 + [VMEM((4, rows, LANES), F32)] * 2
                + [VMEM((rows, LANES), F32)] * 2, after=after)(low, mid, high)


def energy_kernel(blocks_ref, low_ref, mid_ref, high_ref, code_ref, vel_ref, bits_ref, keys_ref, out_ref,
                  buf_ref, pot_ref, mean_ref, table_ref, hot_ref, got_ref):
    received = (low_ref, mid_ref, high_ref)
    rows = bits_ref.shape[0]
    pot_ref[216:256, :] = jnp.zeros((40, LANES), F32)
    mean_ref[216:256, :] = jnp.zeros((40, LANES), F32)
    for cell in range(27):
        ref, within = received[cell // 9], cell % 9
        pot_ref[cell * 8:cell * 8 + 8, :] = ref[within * 16:within * 16 + 8, :]
        mean_ref[cell * 8:cell * 8 + 8, :] = ref[within * 16 + 8:within * 16 + 16, :]
    for k, ref in enumerate((pot_ref, mean_ref)):
        for half in range(2):
            lanes = slice(half * LANES, (half + 1) * LANES)
            flipped = jnp.transpose(ref[lanes, :])
            high = flipped.astype(BF16)
            table_ref[k * 256:k * 256 + 128, lanes] = high
            table_ref[k * 256 + 128:k * 256 + 256, lanes] = (flipped - high.astype(F32)).astype(BF16)
    iota_row = lax.broadcasted_iota(I32, (256, LANES), 0).astype(F32).astype(BF16)
    iota_lane = lax.broadcasted_iota(I32, (LANES, LANES), 0)
    iota_group = lax.broadcasted_iota(I32, (32, LANES), 0)
    one_b, zero_b = jnp.ones((256, LANES), BF16), jnp.zeros((256, LANES), BF16)

    def gather(i, carry):
        here = pl.ds(pl.multiple_of(i * 8, 8), 8)
        code = code_ref[here, :]
        lane = code & 127
        group = code & 31
        at_row = (code >> 7).astype(F32)
        for r in range(8):
            lanes = slice(r * LANES, (r + 1) * LANES)
            want = jnp.broadcast_to(at_row[r:r + 1], (256, LANES)).astype(BF16)
            hot_ref[:, lanes] = jnp.where(iota_row == want, one_b, zero_b)
        for pair in range(4):
            found = jnp.dot(table_ref[...], hot_ref[:, pair * 256:(pair + 1) * 256], preferred_element_type=F32)
            for k in range(2):
                r = pair * 2 + k
                lanes = slice(k * LANES, (k + 1) * LANES)
                pot = found[0:128, lanes] + found[128:256, lanes]
                pot = jnp.where(iota_lane == jnp.broadcast_to(lane[r:r + 1], (LANES, LANES)), pot, 0.0)
                got_ref[0, r:r + 1, :] = jnp.sum(pot, axis=0, keepdims=True)
                at_group = iota_group == jnp.broadcast_to(group[r:r + 1], (32, LANES))
                for c in range(3):
                    o = 256 + c * 32
                    mean = found[o:o + 32, lanes] + found[o + 128:o + 160, lanes]
                    got_ref[1 + c, r:r + 1, :] = jnp.sum(jnp.where(at_group, mean, 0.0), axis=0, keepdims=True)
        kinetic = jnp.zeros((8, LANES), F32)
        for c in range(3):
            diff = vel_ref[c, here, :] - got_ref[1 + c]
            kinetic = kinetic + diff * diff
        buf_ref[pl.ds(pl.multiple_of(i * 8 + 256, 8), 8), :] = got_ref[0] + 0.5 * kinetic
        return carry

    lax.fori_loop(0, blocks_ref[0], gather, 0)
    step_rows = 32
    for stage in reversed(range(STAGES)):
        d = 1 << stage

        def move(i, carry, d=d):
            base = pl.multiple_of((rows // step_rows - 1 - i) * step_rows, step_rows)
            moved = (bits_ref[pl.ds(base, step_rows), :] & d) != 0
            here = pl.ds(pl.multiple_of(base + 256, 8), step_rows)
            buf_ref[here, :] = jnp.where(moved, buf_ref[pl.ds(base + 256 - d, step_rows), :], buf_ref[here, :])
            return carry

        lax.fori_loop(0, rows // step_rows, move, 0)
    out_ref[...] = jnp.where(keys_ref[0:rows, :] < (keys_ref.shape[0] - rows) * LANES * GCAP, buf_ref[pl.ds(256, rows), :], 0.0)


def energies(blocks, low, mid, high, code, vel, bits, table):
    rows = bits.shape[0]
    scratch = [VMEM((rows + 256, LANES), F32), VMEM((256, LANES), F32), VMEM((256, LANES), F32),
               VMEM((512, 256), BF16), VMEM((256, 1024), BF16), VMEM((4, 8, LANES), F32)]
    return call(energy_kernel, [((rows, LANES), F32)], 8, scratch, smem_first=True)(
        blocks, low, mid, high, code, vel, bits, table)[0]


def up(axis, x):
    n = lax.axis_size(axis)
    return lax.ppermute(x, axis, [(i, (i + 1) % n) for i in range(n)])


def down(axis, x):
    n = lax.axis_size(axis)
    return lax.ppermute(x, axis, [((i + 1) % n, i) for i in range(n)])


def local(particles, labels, member_slot, owner_slot):
    slab_all = particles.shape[-1]
    rows = slab_all // LANES
    parts = particles.reshape(7, rows, LANES)
    keys = labels.reshape(rows, LANES) * GCAP + member_slot.reshape(rows, LANES)
    table = jnp.concatenate([keys, owner_slot.reshape(-1, LANES)], axis=0)
    counts = tuple(lax.axis_size(a) for a in ("gx", "gy", "gz"))
    coords = jnp.stack([lax.axis_index(a) for a in ("gx", "gy", "gz")]).astype(I32)
    send_m, keep, send_p, faces, bits, code, vel, n_blocks = members(coords, counts, table, parts)
    from_low = up("gx", send_p)
    from_high = down("gx", send_m)
    near_xy = near((0, 1), parts, (keep,))
    x_all = (from_low, keep, from_high)

    sums = lax.broadcasted_iota(I32, (8, LANES), 0) < 3

    def stack_y(b):
        mom = sum(t[MEMBER_ROWS + 8 * b:MEMBER_ROWS + 8 * b + 8] for t in x_all)
        return [t[b * 96:(b + 1) * 96] for t in x_all] + [jnp.where(sums, mom, near_xy[0:8])]

    y_low = up("gy", jnp.concatenate(stack_y(2) + [faces[1]], axis=0))
    y_high = down("gy", jnp.concatenate(stack_y(0) + [faces[0]], axis=0))
    y_keep = jnp.concatenate(stack_y(1), axis=0)
    near_z = near((2,), parts, (y_keep,))
    edge_x = far(0, parts, near_xy[0:128], from_low[TOP_X:], from_high[TOP_X:], (y_keep,))
    y_all = (y_low, y_keep, y_high)
    mom_z = sum(t[MEMBER_ROWS:TOP] for t in y_all)
    mom_z = jnp.where(sums, mom_z, edge_x[0:8] + near_z[0:8])

    def stack_z(b):
        return [t[(3 * xs + b) * 32:(3 * xs + b + 1) * 32] for t in y_all for xs in range(3)] + [mom_z]

    z_low = up("gz", jnp.concatenate(stack_z(2) + [faces[3]], axis=0))
    z_high = down("gz", jnp.concatenate(stack_z(0) + [faces[2]], axis=0))
    z_keep = jnp.concatenate(stack_z(1), axis=0)
    edge_y = far(1, parts, near_xy[128:256], y_low[TOP:], y_high[TOP:], (z_keep,))
    to_low, stay, to_high = groups(z_low[:TOP], z_keep, z_high[:TOP], (edge_y,))
    edge_z = far(2, parts, near_z, z_low[TOP:], z_high[TOP:], (stay,))
    back_high = down("gz", to_low)
    back_low = up("gz", to_high)
    zs = (back_low, stay, back_high)

    def back_y(b):
        return jnp.concatenate([p for t in zs for p in (t[b * 24:(b + 1) * 24], t[72:80])], axis=0)

    ylow = up("gy", back_y(2))
    yhigh = down("gy", back_y(0))
    ys = (ylow, back_y(1), yhigh)

    def back_x(b):
        return jnp.concatenate(
            [p for z in range(3) for t in ys
             for p in (t[z * 32 + b * 8:z * 32 + b * 8 + 8], t[z * 32 + 24:z * 32 + 32])], axis=0)

    xlow = up("gx", back_x(2))
    xhigh = down("gx", back_x(0))
    energy = energies(n_blocks, xlow, back_x(1), xhigh, code, vel, bits, table)
    edge = jnp.concatenate([edge_x, edge_y, edge_z], axis=0)
    return edge.reshape(1, 1, 1, slab_all), energy.reshape(1, 1, 1, slab_all)


def solution(mesh):
    return jax.shard_map(
        local,
        mesh=mesh,
        in_specs=(
            P(None, "gx", "gy", "gz", None),
            P("gx", "gy", "gz", None),
            P("gx", "gy", "gz", None),
            P(),
        ),
        out_specs=(P("gx", "gy", "gz", None), P("gx", "gy", "gz", None)),
        check_vma=False,
    )
```

```python
import functools

import jax
import jax.numpy as jnp
from jax import lax
from jax.experimental import pallas as pl
from jax.experimental.pallas import tpu as pltpu
from jax.sharding import PartitionSpec as P

TG = 8
GCAP = 32
LANES = 128
SOFTENING = 0.01
EDGE_COUPLING = 1.0 / 256.0
GROUP_COUPLING = 1.0 / 16.0
VMEM_LIMIT = 32 * 1024 * 1024
MEMBER_ROWS = 9 * 32
TOP = MEMBER_ROWS + 8
TOP_X = MEMBER_ROWS + 24
VMEM = pltpu.VMEM
F32 = jnp.float32
BF16 = jnp.bfloat16
I32 = jnp.int32


def call(kernel, outs, n_in, scratch, smem_first=False, after=()):
    after = tuple(a[0:8] for a in after)
    specs = [pl.BlockSpec(memory_space=VMEM)] * n_in + [pl.BlockSpec(memory_space=VMEM)] * len(after)
    if smem_first:
        specs[0] = pl.BlockSpec(memory_space=pltpu.SMEM)

    def body(*refs):
        kernel(*refs[:n_in], *refs[n_in + len(after):])

    run = pl.pallas_call(
        body,
        out_shape=[jax.ShapeDtypeStruct(s, d) for s, d in outs],
        in_specs=specs,
        out_specs=[pl.BlockSpec(memory_space=VMEM)] * len(outs),
        scratch_shapes=scratch,
        compiler_params=pltpu.CompilerParams(vmem_limit_bytes=VMEM_LIMIT),
    )
    return lambda *args: run(*args, *after)


def row(ref, index):
    return jnp.broadcast_to(ref[pl.ds(index, 1), :], (8, LANES))


def take_lanes(values, index):
    return jnp.take_along_axis(values, index, axis=1, mode="promise_in_bounds")


STAGES = 9
INVALID = (4096 * 32) << STAGES
PAD = 16
NT = (((1,), (1,)), ((), ()))


def owner_offset(mine, theirs, n):
    if n & (n - 1):
        step = (mine - theirs + n // 2 + n) % n - n // 2
    else:
        step = ((mine - theirs + n // 2) & (n - 1)) - n // 2
    return 1 - step


def member_kernel(counts, coords, table_hbm, parts_hbm,
                  out_m, out_0, out_p, faces_ref, bits_ref, code_ref, vel_ref, blocks_ref,
                  word_ref, buf_ref, table_ref, cell_ref, lhs_a, lhs_b, rhs_a, rhs_b,
                  lhs2_a, lhs2_b, rhs2_a, rhs2_b, acc_ref, acc2_ref, sems):
    rows = parts_hbm.shape[1]
    owner_ref = table_ref.at[pl.ds(rows, table_ref.shape[0] - rows), :]
    ngroups = owner_ref.shape[0] * LANES
    copies = [
        pltpu.make_async_copy(table_hbm, table_ref, sems.at[0]),
        pltpu.make_async_copy(parts_hbm, buf_ref.at[:, pl.ds(0, rows), :], sems.at[1]),
    ]
    for copy in copies:
        copy.start()
    word_ref[pl.ds(rows, 256), :] = jnp.full((256, LANES), INVALID, I32)
    acc_ref[...] = jnp.zeros_like(acc_ref)
    acc2_ref[...] = jnp.zeros_like(acc2_ref)
    bits_ref[...] = jnp.zeros_like(bits_ref)
    for c in range(7):
        buf_ref[c, pl.ds(rows, PAD), :] = jnp.zeros((PAD, LANES), F32)
    below = lax.broadcasted_iota(I32, (rows, rows), 0) > lax.broadcasted_iota(I32, (rows, rows), 1)
    below = jnp.where(below, 1.0, 0.0).astype(BF16)
    copies[0].wait()
    keys = table_ref[0:rows, :]
    member = keys < ngroups * GCAP
    flags = jnp.where(member, 1.0, 0.0)
    rank = jnp.dot(below, flags.astype(BF16), preferred_element_type=F32)
    place = lax.broadcasted_iota(I32, (rows, LANES), 0)
    shift = place - rank.astype(I32)
    word = (keys << STAGES) | shift
    word_ref[pl.ds(0, rows), :] = jnp.where(member, word, INVALID)
    tops = jnp.max(rank + flags, axis=0, keepdims=True)
    n_blocks = (jnp.max(tops).astype(I32) + 7) // 8
    blocks_ref[0] = n_blocks
    copies[1].wait()
    tiles = TG * TG
    for out, face in ((out_m, 0), (out_p, 1)):
        for k, c in enumerate((0, 1, 2, 6)):
            out[TOP_X + k * tiles:TOP_X + (k + 1) * tiles, :] = buf_ref[c, face * tiles:(face + 1) * tiles, :]
    for face in range(2, 6):
        for k, c in enumerate((0, 1, 2, 6)):
            faces_ref[face - 2, k * tiles:(k + 1) * tiles, :] = buf_ref[c, face * tiles:(face + 1) * tiles, :]
    step_rows = 32
    for stage in range(STAGES):
        d = 1 << stage

        def move(i, carry, d=d):
            base = pl.multiple_of(i * step_rows, step_rows)
            here = pl.ds(base, step_rows)
            there = pl.ds(base + d, step_rows)
            own = word_ref[here, :]
            far = word_ref[there, :]
            bits_ref[here, :] = bits_ref[here, :] | (own & d)
            comes = (far & d) != 0
            goes = (own & d) != 0
            word_ref[here, :] = jnp.where(comes, far, jnp.where(goes, INVALID, own))
            for c in range(7):
                buf_ref[c, here, :] = jnp.where(comes, buf_ref[c, there, :], buf_ref[c, here, :])
            return carry

        lax.fori_loop(0, rows // step_rows, move, 0)

    iota32 = lax.broadcasted_iota(I32, (32, LANES), 0)
    iota_b = iota32.astype(F32).astype(BF16)
    zero_b = jnp.zeros((32, LANES), BF16)
    one_b = jnp.ones((32, LANES), BF16)

    def decode(i, carry):
        here = pl.ds(pl.multiple_of(i * PAD, PAD), PAD)
        key = word_ref[here, :] >> STAGES
        valid = key < ngroups * GCAP
        lab = key >> 5
        slot = key & 31
        low = lab & 127
        high = lab >> 7
        owner = jnp.zeros((PAD, LANES), I32)
        for r in range(ngroups // LANES):
            found = take_lanes(jnp.broadcast_to(owner_ref[pl.ds(r, 1), :], (PAD, LANES)), low)
            owner = jnp.where(high == r, found, owner)
        group = owner & 31
        device = owner >> 5
        nx, ny, nz = counts
        ox = owner_offset(coords[0], device // (nz * ny), nx)
        oy = owner_offset(coords[1], device // nz % ny, ny)
        oz = owner_offset(coords[2], device % nz, nz)
        cell_ref[here, :] = jnp.where(valid, (ox * 3 + oy) * 3 + oz, -1).astype(F32)
        code = (((ox * 9 + oz * 3 + oy) * 8 + (slot & 7)) << 7) | ((slot >> 3) << 5) | group
        code_ref[here, :] = jnp.where(valid, code, 0)
        return carry

    lax.fori_loop(0, jnp.minimum((n_blocks + 4) // 2, (rows + PAD) // PAD), decode, 0)

    def build(i, lhs, rhs, lhs2, rhs2):
        here = pl.ds(pl.multiple_of(i * 8, 8), 8)
        cell = cell_ref[here, :]
        code = code_ref[here, :]
        slot = (((code >> 5) & 3) << 3) | ((code >> 7) & 7)
        group = code & 31
        mass = buf_ref[6, here, :]
        vals = [buf_ref[c, here, :] - 0.5 * TG for c in range(3)] + [mass]
        for c in range(3):
            v = buf_ref[3 + c, here, :]
            vel_ref[c, here, :] = v
            vals.append(mass * v)
        high_part = [v.astype(BF16).astype(F32) for v in vals]
        low_part = [v - h for v, h in zip(vals, high_part)]
        slot_f, group_f = slot.astype(F32), group.astype(F32)

        def spread(v, r):
            return jnp.broadcast_to(v[r:r + 1], (32, LANES)).astype(BF16)

        for r in range(8):
            lanes = slice(r * LANES, (r + 1) * LANES)
            at_group = iota_b == spread(group_f, r)
            at_slot = iota_b == spread(slot_f, r)
            cell_r = spread(cell, r)
            hot = jnp.where(at_group, one_b, zero_b)
            for d in range(27):
                lhs[d * 32:(d + 1) * 32, lanes] = jnp.where(cell_r == jnp.asarray(d, BF16), hot, zero_b)
            lhs2[:, lanes] = jnp.where(iota_b == cell_r, one_b, zero_b)
            for half, parts in ((0, high_part), (1, low_part)):
                for c in range(4):
                    o = half * 128 + c * 32
                    rhs[o:o + 32, lanes] = jnp.where(at_slot, spread(parts[c], r), zero_b)
                for c in range(3):
                    o = half * 96 + c * 32
                    rhs2[o:o + 32, lanes] = jnp.where(at_group, spread(parts[4 + c], r), zero_b)

    def add(lhs, rhs, lhs2, rhs2):
        acc_ref[...] += lax.dot_general(lhs[...], rhs[...], NT, preferred_element_type=F32)
        acc2_ref[0:32, :] += lax.dot_general(lhs2[...], rhs2[...], NT, preferred_element_type=F32)

    slot_a = (lhs_a, rhs_a, lhs2_a, rhs2_a)
    slot_b = (lhs_b, rhs_b, lhs2_b, rhs2_b)
    build(0, *slot_a)

    def scatter(i, carry):
        build(2 * i + 1, *slot_b)
        add(*slot_a)
        build(2 * i + 2, *slot_a)
        add(*slot_b)
        return carry

    lax.fori_loop(0, (n_blocks + 1) // 2, scatter, 0)
    for a, out in enumerate((out_m, out_0, out_p)):
        out[0:288, :] = acc_ref[a * 288:(a + 1) * 288, 0:128] + acc_ref[a * 288:(a + 1) * 288, 128:256]
        for b in range(3):
            at = slice(MEMBER_ROWS + 8 * b, MEMBER_ROWS + 8 * b + 8)
            first = a * 9 + b * 3
            mom = acc2_ref[first:first + 8, 0:96] + acc2_ref[first:first + 8, 96:192]
            out[at, :] = jnp.concatenate([mom, jnp.zeros((8, 32), F32)], axis=1)


def members(coords, counts, table, parts):
    rows = parts.shape[1]
    send = (TOP_X + 4 * TG * TG, LANES)

    def kernel(coords_ref, *rest):
        member_kernel(counts, [coords_ref[k] for k in range(3)], *rest)

    shapes = [(send, F32), ((TOP_X, LANES), F32), (send, F32), ((4, 4 * TG * TG, LANES), F32), ((rows, LANES), I32),
              ((rows + PAD, LANES), I32), ((3, rows + PAD, LANES), F32), ((1,), I32)]
    specs = [pl.BlockSpec(memory_space=VMEM)] * 8
    specs[7] = pl.BlockSpec(memory_space=pltpu.SMEM)
    return pl.pallas_call(
        kernel,
        out_shape=[jax.ShapeDtypeStruct(s, d) for s, d in shapes],
        in_specs=[pl.BlockSpec(memory_space=m) for m in [pltpu.SMEM] + [pltpu.HBM] * 2],
        out_specs=specs,
        scratch_shapes=[
            VMEM((rows + 256, LANES), I32),
            VMEM((7, rows + 256, LANES), F32),
            VMEM(table.shape, I32),
            VMEM((rows + PAD, LANES), F32),
        ] + [VMEM((27 * 32, 1024), BF16)] * 2 + [VMEM((256, 1024), BF16)] * 2
        + [VMEM((32, 1024), BF16)] * 2 + [VMEM((192, 1024), BF16)] * 2 + [
            VMEM((27 * 32, 256), F32),
            VMEM((40, 192), F32),
            pltpu.SemaphoreType.DMA((2,)),
        ],
        compiler_params=pltpu.CompilerParams(vmem_limit_bytes=VMEM_LIMIT),
    )(coords, table, parts)


def inverse_distance(target, source):
    dx = target[0] - source[0]
    dy = target[1] - source[1]
    dz = target[2] - source[2]
    return lax.rsqrt(dx * dx + dy * dy + (dz * dz + SOFTENING))


def sym_pairs(target, acc, source, base, first, offsets, once=(), skip_self=False, lone=()):
    src = [[row(ref, base + first + r) for ref in source] for r in range(4)]
    gains = [jnp.zeros((8, LANES), F32) for _ in range(4)]
    sublane = lax.broadcasted_iota(I32, (8, LANES), 0)
    for t in list(offsets) + list(lone):
        at = pl.ds(pl.multiple_of(base + 8 * t, 8), 8)
        tgt = [ref[at, :] for ref in target]
        total = acc[at, :]
        for r in range(4):
            inv = inverse_distance(tgt, src[r])
            mine = inv * src[r][3]
            if skip_self and t == 0:
                mine = jnp.where(sublane == first + r, 0.0, mine)
            total = total + mine
            if t in offsets:
                gains[r] = gains[r] + inv * tgt[3]
        acc[at, :] = total
    return [jnp.sum(g, axis=0, keepdims=True) for g in gains]


def near_kernel(axes, parts_ref, out_ref, xs, ys, zs, ms, acc):
    target = (xs, ys, zs, ms)
    tiles = 2 * TG * TG
    for k, axis in enumerate(axes):
        for ref, c in zip(target, (0, 1, 2, 6)):
            t = jnp.transpose(parts_ref[c, axis * tiles:(axis + 1) * tiles, :])
            ref[0:128, :] = t
            ref[128:256, :] = t
        acc[...] = jnp.zeros_like(acc)

        def body(jb, carry):
            base = pl.multiple_of(jb * 8, 8)
            for first in (0, 4):
                gains = sym_pairs(target, acc, target, base, first, range(1, 8), skip_self=True, lone=(0, 8))
                for r in range(4):
                    at = pl.ds(base + first + r, 1)
                    acc[at, :] = acc[at, :] + gains[r]
            return carry

        lax.fori_loop(0, 16, body, 0)
        out_ref[k * 128:(k + 1) * 128, :] = acc[0:128, :] + acc[128:256, :]


def far_kernel(axis, n_done, parts_ref, near_ref, low_ref, high_ref, *rest):
    done, (out_ref, xs, ys, zs, ms, acc) = rest[:n_done], rest[n_done:]
    for k, ref in enumerate(done):
        out_ref[k * 128:(k + 1) * 128, :] = ref[...]
    tiles = TG * TG
    source = (xs, ys, zs, ms)
    target = []
    for k, (ref, c) in enumerate(zip(source, (0, 1, 2, 6))):
        low = low_ref[k * tiles:(k + 1) * tiles, :]
        high = high_ref[k * tiles:(k + 1) * tiles, :]
        if k == axis:
            low = low - 1.0 * TG
            high = high + 1.0 * TG
        ref[...] = jnp.transpose(jnp.concatenate([low, high], axis=0))
    tgt_refs = acc
    for k, c in enumerate((0, 1, 2)):
        tgt_refs[k, :, :] = jnp.transpose(parts_ref[c, axis * 2 * tiles:(axis + 1) * 2 * tiles, :])
    tgt_refs[3, :, :] = near_ref[...]

    def body(jb, carry):
        base = pl.multiple_of(jb * 4, 4)
        src = [[row(ref, base + r) for ref in source] for r in range(4)]
        for t in range(16):
            at = slice(8 * t, 8 * t + 8)
            tgt = [tgt_refs[k, at, :] for k in range(3)]
            total = tgt_refs[3, at, :]
            for r in range(4):
                total = total + inverse_distance(tgt, src[r]) * src[r][3]
            tgt_refs[3, at, :] = total
        return carry

    lax.fori_loop(0, 32, body, 0)
    out_ref[n_done * 128:(n_done + 1) * 128, :] = jnp.transpose(tgt_refs[3, :, :]) * (-EDGE_COUPLING)


def near(axes, parts, after):
    return call(functools.partial(near_kernel, axes), [((128 * len(axes), LANES), F32)], 1,
                [VMEM((256, LANES), F32)] * 5, after=after)(parts)[0]


def far(axis, parts, near_part, low, high, after=(), done=()):
    return call(functools.partial(far_kernel, axis, len(done)), [((128 * (len(done) + 1), LANES), F32)],
                4 + len(done), [VMEM((128, LANES), F32)] * 4 + [VMEM((4, 128, LANES), F32)], after=after)(
                    parts, near_part, low, high, *done)[0]


def group_kernel(low_ref, mid_ref, high_ref, out_m, out_0, out_p,
                 x0, y0, z0, m0, acc, s1, s2, g1, g2):
    base = (x0, y0, z0, m0)
    n_rows = 27 * 8
    quarter = lax.broadcasted_iota(I32, (8, LANES), 1) // 32
    received = (low_ref, mid_ref, high_ref)
    mom = jnp.zeros((8, LANES), F32)
    cells = []
    for e in range(28):
        if e == 27:
            cells.append(jnp.zeros((32, LANES), F32))
        else:
            ref, within = received[e // 9], e % 9
            cells.append(ref[within * 32:within * 32 + 32, :])
    for ref, dz in zip(received, (2, 1, 0)):
        mom = mom + jnp.broadcast_to(ref[MEMBER_ROWS + dz:MEMBER_ROWS + dz + 1, :], (8, LANES))
    for blk in range(7):
        flat = jnp.transpose(jnp.concatenate(cells[blk * 4:blk * 4 + 4], axis=0))
        for c in range(4):
            quads = [flat[c * 32 + q * 8:c * 32 + q * 8 + 8, :] for q in range(4)]
            for a in range(4):
                e = blk * 4 + a
                if e == 27:
                    continue
                mixed = None
                for q in range(4):
                    moved = quads[q] if q == a else pltpu.roll(quads[q], (32 * (q - a)) % 128, 1)
                    mixed = moved if mixed is None else jnp.where(quarter == q, moved, mixed)
                if c < 3:
                    d = (e % 3, e // 3 % 3, e // 9)[c] - 1
                    mixed = mixed + float(TG * d)
                base[c][e * 8:e * 8 + 8, :] = mixed
                base[c][n_rows + e * 8:n_rows + e * 8 + 8, :] = mixed
    for c in range(4):
        v = base[c][0:n_rows, :]
        s1[c, :, :] = pltpu.roll(v, 96, 1)
        s2[c, :, :] = pltpu.roll(v, 64, 1)
    acc[...] = jnp.zeros_like(acc)
    src1 = tuple(s1.at[c] for c in range(4))
    src2 = tuple(s2.at[c] for c in range(4))

    def body(jb, carry):
        at0 = pl.multiple_of(jb * 8, 8)
        for first in (0, 4):
            own = sym_pairs(base, acc, base, at0, first, range(1, 14), skip_self=True, lone=(0,))
            one = sym_pairs(base, acc, src1, at0, first, range(0, 27))
            two = sym_pairs(base, acc, src2, at0, first, range(1, 14), lone=(0,))
            for r in range(4):
                at = pl.ds(at0 + first + r, 1)
                acc[at, :] = acc[at, :] + own[r]
                g1[at, :] = one[r]
                g2[at, :] = two[r]
        return carry

    lax.fori_loop(0, 27, body, 0)
    total = (acc[0:n_rows, :] + acc[n_rows:2 * n_rows, :]
             + pltpu.roll(g1[...], 32, 1) + pltpu.roll(g2[...], 64, 1))
    mass = jnp.sum(m0[0:n_rows, :], axis=0, keepdims=True)
    mass = jnp.broadcast_to(mass, (8, LANES))
    mass = mass + pltpu.roll(mass, 32, 1)
    mass = mass + pltpu.roll(mass, 64, 1)
    mean = mom / mass
    for zs, out in enumerate((out_m, out_0, out_p)):
        out[0:72, :] = total[zs * 72:(zs + 1) * 72, :] * (-GROUP_COUPLING)
        out[72:80, :] = mean


def groups(low, mid, high, after):
    rows = 27 * 8
    return call(group_kernel, [((80, LANES), F32)] * 3, 3,
                [VMEM((2 * rows, LANES), F32)] * 5 + [VMEM((4, rows, LANES), F32)] * 2
                + [VMEM((rows, LANES), F32)] * 2, after=after)(low, mid, high)


def energy_kernel(blocks_ref, low_ref, mid_ref, high_ref, code_ref, vel_ref, bits_ref, keys_ref, out_ref,
                  buf_ref, pot_ref, mean_ref, table_ref, hot_a, hot_b, got_a, got_b):
    received = (low_ref, mid_ref, high_ref)
    rows = bits_ref.shape[0]
    pot_ref[216:256, :] = jnp.zeros((40, LANES), F32)
    mean_ref[216:256, :] = jnp.zeros((40, LANES), F32)
    for cell in range(27):
        ref, within = received[cell // 9], cell % 9
        pot_ref[cell * 8:cell * 8 + 8, :] = ref[within * 16:within * 16 + 8, :]
        mean_ref[cell * 8:cell * 8 + 8, :] = ref[within * 16 + 8:within * 16 + 16, :]
    for k, ref in enumerate((pot_ref, mean_ref)):
        for half in range(2):
            lanes = slice(half * LANES, (half + 1) * LANES)
            flipped = jnp.transpose(ref[lanes, :])
            high = flipped.astype(BF16)
            low = (flipped - high.astype(F32)).astype(BF16)
            base, size = ((0, 128), (256, 96))[k]
            table_ref[base:base + size, lanes] = high[0:size]
            table_ref[base + size:base + 2 * size, lanes] = low[0:size]
    iota_row = lax.broadcasted_iota(I32, (224, LANES), 0).astype(F32).astype(BF16)
    iota_lane = lax.broadcasted_iota(I32, (LANES, LANES), 0)
    iota_group = lax.broadcasted_iota(I32, (32, LANES), 0)
    one_b, zero_b = jnp.ones((224, LANES), BF16), jnp.zeros((224, LANES), BF16)
    hot_a[224:256, :] = jnp.zeros((32, 1024), BF16)
    hot_b[224:256, :] = jnp.zeros((32, 1024), BF16)

    def mark(i, hot_ref):
        at_row = (code_ref[pl.ds(pl.multiple_of(i * 8, 8), 8), :] >> 7).astype(F32)
        for r in range(8):
            lanes = slice(r * LANES, (r + 1) * LANES)
            want = jnp.broadcast_to(at_row[r:r + 1], (224, LANES)).astype(BF16)
            hot_ref[0:224, lanes] = jnp.where(iota_row == want, one_b, zero_b)

    def fetch(i, hot_ref, got_ref):
        here = pl.ds(pl.multiple_of(i * 8, 8), 8)
        code = code_ref[here, :]
        lane = code & 127
        group = code & 31
        for pair in range(4):
            found = jnp.dot(table_ref[...], hot_ref[:, pair * 256:(pair + 1) * 256], preferred_element_type=F32)
            for k in range(2):
                r = pair * 2 + k
                lanes = slice(k * LANES, (k + 1) * LANES)
                pot = found[0:128, lanes] + found[128:256, lanes]
                pot = jnp.where(iota_lane == jnp.broadcast_to(lane[r:r + 1], (LANES, LANES)), pot, 0.0)
                got_ref[0, r:r + 1, :] = jnp.sum(pot, axis=0, keepdims=True)
                at_group = iota_group == jnp.broadcast_to(group[r:r + 1], (32, LANES))
                for c in range(3):
                    o = 256 + c * 32
                    mean = found[o:o + 32, lanes] + found[o + 96:o + 128, lanes]
                    got_ref[1 + c, r:r + 1, :] = jnp.sum(jnp.where(at_group, mean, 0.0), axis=0, keepdims=True)
        kinetic = jnp.zeros((8, LANES), F32)
        for c in range(3):
            diff = vel_ref[c, here, :] - got_ref[1 + c]
            kinetic = kinetic + diff * diff
        buf_ref[pl.ds(pl.multiple_of(i * 8 + 256, 8), 8), :] = got_ref[0] + 0.5 * kinetic

    mark(0, hot_a)

    def gather(i, carry):
        mark(2 * i + 1, hot_b)
        fetch(2 * i, hot_a, got_a)
        mark(2 * i + 2, hot_a)
        fetch(2 * i + 1, hot_b, got_b)
        return carry

    lax.fori_loop(0, (blocks_ref[0] + 1) // 2, gather, 0)
    step_rows = 32
    for stage in reversed(range(STAGES)):
        d = 1 << stage

        def move(i, carry, d=d):
            base = pl.multiple_of((rows // step_rows - 1 - i) * step_rows, step_rows)
            moved = (bits_ref[pl.ds(base, step_rows), :] & d) != 0
            here = pl.ds(pl.multiple_of(base + 256, 8), step_rows)
            buf_ref[here, :] = jnp.where(moved, buf_ref[pl.ds(base + 256 - d, step_rows), :], buf_ref[here, :])
            return carry

        lax.fori_loop(0, rows // step_rows, move, 0)
    out_ref[...] = jnp.where(keys_ref[0:rows, :] < (keys_ref.shape[0] - rows) * LANES * GCAP, buf_ref[pl.ds(256, rows), :], 0.0)


def energies(blocks, low, mid, high, code, vel, bits, table):
    rows = bits.shape[0]
    scratch = [VMEM((rows + 256, LANES), F32), VMEM((256, LANES), F32), VMEM((256, LANES), F32),
               VMEM((448, 256), BF16)] + [VMEM((256, 1024), BF16)] * 2 + [VMEM((4, 8, LANES), F32)] * 2
    return call(energy_kernel, [((rows, LANES), F32)], 8, scratch, smem_first=True)(
        blocks, low, mid, high, code, vel, bits, table)[0]


def up(axis, x):
    n = lax.axis_size(axis)
    return lax.ppermute(x, axis, [(i, (i + 1) % n) for i in range(n)])


def down(axis, x):
    n = lax.axis_size(axis)
    return lax.ppermute(x, axis, [((i + 1) % n, i) for i in range(n)])


def local(particles, labels, member_slot, owner_slot):
    slab_all = particles.shape[-1]
    rows = slab_all // LANES
    parts = particles.reshape(7, rows, LANES)
    keys = labels.reshape(rows, LANES) * GCAP + member_slot.reshape(rows, LANES)
    table = jnp.concatenate([keys, owner_slot.reshape(-1, LANES)], axis=0)
    counts = tuple(lax.axis_size(a) for a in ("gx", "gy", "gz"))
    coords = jnp.stack([lax.axis_index(a) for a in ("gx", "gy", "gz")]).astype(I32)
    send_m, keep, send_p, faces, bits, code, vel, n_blocks = members(coords, counts, table, parts)
    from_low = up("gx", send_p)
    from_high = down("gx", send_m)
    near_xy = near((0, 1), parts, (keep,))
    x_all = (from_low, keep, from_high)

    sums = lax.broadcasted_iota(I32, (8, LANES), 0) < 3

    def stack_y(b):
        mom = sum(t[MEMBER_ROWS + 8 * b:MEMBER_ROWS + 8 * b + 8] for t in x_all)
        return [t[b * 96:(b + 1) * 96] for t in x_all] + [jnp.where(sums, mom, near_xy[0:8])]

    y_low = up("gy", jnp.concatenate(stack_y(2) + [faces[1]], axis=0))
    y_high = down("gy", jnp.concatenate(stack_y(0) + [faces[0]], axis=0))
    y_keep = jnp.concatenate(stack_y(1), axis=0)
    near_z = near((2,), parts, (y_keep,))
    edge_x = far(0, parts, near_xy[0:128], from_low[TOP_X:], from_high[TOP_X:], (y_keep,))
    y_all = (y_low, y_keep, y_high)
    mom_z = sum(t[MEMBER_ROWS:TOP] for t in y_all)
    mom_z = jnp.where(sums, mom_z, edge_x[0:8] + near_z[0:8])

    def stack_z(b):
        return [t[(3 * xs + b) * 32:(3 * xs + b + 1) * 32] for t in y_all for xs in range(3)] + [mom_z]

    z_low = up("gz", jnp.concatenate(stack_z(2) + [faces[3]], axis=0))
    z_high = down("gz", jnp.concatenate(stack_z(0) + [faces[2]], axis=0))
    z_keep = jnp.concatenate(stack_z(1), axis=0)
    edge_y = far(1, parts, near_xy[128:256], y_low[TOP:], y_high[TOP:], (z_keep,))
    to_low, stay, to_high = groups(z_low[:TOP], z_keep, z_high[:TOP], (edge_y,))
    edge = far(2, parts, near_z, z_low[TOP:], z_high[TOP:], (stay,), (edge_x, edge_y))
    back_high = down("gz", to_low)
    back_low = up("gz", to_high)
    zs = (back_low, stay, back_high)

    def back_y(b):
        return jnp.concatenate([p for t in zs for p in (t[b * 24:(b + 1) * 24], t[72:80])], axis=0)

    ylow = up("gy", back_y(2))
    yhigh = down("gy", back_y(0))
    ys = (ylow, back_y(1), yhigh)

    def back_x(b):
        return jnp.concatenate(
            [p for z in range(3) for t in ys
             for p in (t[z * 32 + b * 8:z * 32 + b * 8 + 8], t[z * 32 + 24:z * 32 + 32])], axis=0)

    xlow = up("gx", back_x(2))
    xhigh = down("gx", back_x(0))
    energy = energies(n_blocks, xlow, back_x(1), xhigh, code, vel, bits, table)
    return edge.reshape(1, 1, 1, slab_all), energy.reshape(1, 1, 1, slab_all)


def solution(mesh):
    return jax.shard_map(
        local,
        mesh=mesh,
        in_specs=(
            P(None, "gx", "gy", "gz", None),
            P("gx", "gy", "gz", None),
            P("gx", "gy", "gz", None),
            P(),
        ),
        out_specs=(P("gx", "gy", "gz", None), P("gx", "gy", "gz", None)),
        check_vma=False,
    )
```

```python
import functools

import jax
import jax.numpy as jnp
from jax import lax
from jax.experimental import pallas as pl
from jax.experimental.pallas import tpu as pltpu
from jax.sharding import PartitionSpec as P

TG = 8
GCAP = 32
LANES = 128
SOFTENING = 0.01
EDGE_COUPLING = 1.0 / 256.0
GROUP_COUPLING = 1.0 / 16.0
VMEM_LIMIT = 32 * 1024 * 1024
MEMBER_ROWS = 9 * 32
TOP = MEMBER_ROWS + 8
TOP_X = MEMBER_ROWS + 24
VMEM = pltpu.VMEM
F32 = jnp.float32
BF16 = jnp.bfloat16
I32 = jnp.int32


def call(kernel, outs, n_in, scratch, smem_first=False, after=()):
    after = tuple(a[0:8] for a in after)
    specs = [pl.BlockSpec(memory_space=VMEM)] * n_in + [pl.BlockSpec(memory_space=VMEM)] * len(after)
    if smem_first:
        specs[0] = pl.BlockSpec(memory_space=pltpu.SMEM)

    def body(*refs):
        kernel(*refs[:n_in], *refs[n_in + len(after):])

    run = pl.pallas_call(
        body,
        out_shape=[jax.ShapeDtypeStruct(s, d) for s, d in outs],
        in_specs=specs,
        out_specs=[pl.BlockSpec(memory_space=VMEM)] * len(outs),
        scratch_shapes=scratch,
        compiler_params=pltpu.CompilerParams(vmem_limit_bytes=VMEM_LIMIT),
    )
    return lambda *args: run(*args, *after)


def row(ref, index):
    return jnp.broadcast_to(ref[pl.ds(index, 1), :], (8, LANES))


def take_lanes(values, index):
    return jnp.take_along_axis(values, index, axis=1, mode="promise_in_bounds")


STAGES = 9
INVALID = (4096 * 32) << STAGES
PAD = 16
NT = (((1,), (1,)), ((), ()))


def owner_offset(mine, theirs, n):
    if n & (n - 1):
        step = (mine - theirs + n // 2 + n) % n - n // 2
    else:
        step = ((mine - theirs + n // 2) & (n - 1)) - n // 2
    return 1 - step


def member_kernel(counts, coords, table_hbm, parts_hbm,
                  out_m, out_0, out_p, faces_ref, bits_ref, code_ref, vel_ref, blocks_ref,
                  word_ref, buf_ref, table_ref, cell_ref, lhs_a, lhs_b, rhs_a, rhs_b,
                  lhs2_a, lhs2_b, rhs2_a, rhs2_b, acc_ref, acc2_ref, sems):
    rows = parts_hbm.shape[1]
    owner_ref = table_ref.at[pl.ds(rows, table_ref.shape[0] - rows), :]
    ngroups = owner_ref.shape[0] * LANES
    copies = [
        pltpu.make_async_copy(table_hbm, table_ref, sems.at[0]),
        pltpu.make_async_copy(parts_hbm, buf_ref.at[:, pl.ds(0, rows), :], sems.at[1]),
    ]
    for copy in copies:
        copy.start()
    word_ref[pl.ds(rows, 256), :] = jnp.full((256, LANES), INVALID, I32)
    acc_ref[...] = jnp.zeros_like(acc_ref)
    acc2_ref[...] = jnp.zeros_like(acc2_ref)
    bits_ref[...] = jnp.zeros_like(bits_ref)
    for c in range(7):
        buf_ref[c, pl.ds(rows, PAD), :] = jnp.zeros((PAD, LANES), F32)
    below = lax.broadcasted_iota(I32, (rows, rows), 0) > lax.broadcasted_iota(I32, (rows, rows), 1)
    below = jnp.where(below, 1.0, 0.0).astype(BF16)
    copies[0].wait()
    keys = table_ref[0:rows, :]
    member = keys < ngroups * GCAP
    flags = jnp.where(member, 1.0, 0.0)
    rank = jnp.dot(below, flags.astype(BF16), preferred_element_type=F32)
    place = lax.broadcasted_iota(I32, (rows, LANES), 0)
    shift = place - rank.astype(I32)
    word = (keys << STAGES) | shift
    word_ref[pl.ds(0, rows), :] = jnp.where(member, word, INVALID)
    tops = jnp.max(rank + flags, axis=0, keepdims=True)
    n_blocks = (jnp.max(tops).astype(I32) + 7) // 8
    blocks_ref[0] = n_blocks
    copies[1].wait()
    tiles = TG * TG
    for out, face in ((out_m, 0), (out_p, 1)):
        for k, c in enumerate((0, 1, 2, 6)):
            out[TOP_X + k * tiles:TOP_X + (k + 1) * tiles, :] = buf_ref[c, face * tiles:(face + 1) * tiles, :]
    for face in range(2, 6):
        for k, c in enumerate((0, 1, 2, 6)):
            faces_ref[face - 2, k * tiles:(k + 1) * tiles, :] = buf_ref[c, face * tiles:(face + 1) * tiles, :]
    step_rows = 32
    for stage in range(STAGES):
        d = 1 << stage

        def move(i, carry, d=d):
            base = pl.multiple_of(i * step_rows, step_rows)
            here = pl.ds(base, step_rows)
            there = pl.ds(base + d, step_rows)
            own = word_ref[here, :]
            far = word_ref[there, :]
            bits_ref[here, :] = bits_ref[here, :] | (own & d)
            comes = (far & d) != 0
            goes = (own & d) != 0
            word_ref[here, :] = jnp.where(comes, far, jnp.where(goes, INVALID, own))
            for c in range(7):
                buf_ref[c, here, :] = jnp.where(comes, buf_ref[c, there, :], buf_ref[c, here, :])
            return carry

        lax.fori_loop(0, rows // step_rows, move, 0)

    iota32 = lax.broadcasted_iota(I32, (32, LANES), 0)
    iota_b = iota32.astype(F32).astype(BF16)
    zero_b = jnp.zeros((32, LANES), BF16)
    one_b = jnp.ones((32, LANES), BF16)

    def decode(i, carry):
        here = pl.ds(pl.multiple_of(i * PAD, PAD), PAD)
        key = word_ref[here, :] >> STAGES
        valid = key < ngroups * GCAP
        lab = key >> 5
        slot = key & 31
        low = lab & 127
        high = lab >> 7
        owner = jnp.zeros((PAD, LANES), I32)
        for r in range(ngroups // LANES):
            found = take_lanes(jnp.broadcast_to(owner_ref[pl.ds(r, 1), :], (PAD, LANES)), low)
            owner = jnp.where(high == r, found, owner)
        group = owner & 31
        device = owner >> 5
        nx, ny, nz = counts
        ox = owner_offset(coords[0], device // (nz * ny), nx)
        oy = owner_offset(coords[1], device // nz % ny, ny)
        oz = owner_offset(coords[2], device % nz, nz)
        cell_ref[here, :] = jnp.where(valid, (ox * 3 + oy) * 3 + oz, -1).astype(F32)
        code = (((ox * 9 + oz * 3 + oy) * 8 + (slot & 7)) << 7) | ((slot >> 3) << 5) | group
        code_ref[here, :] = jnp.where(valid, code, 0)
        return carry

    lax.fori_loop(0, jnp.minimum((n_blocks + 4) // 2, (rows + PAD) // PAD), decode, 0)

    def build(i, lhs, rhs, lhs2, rhs2):
        here = pl.ds(pl.multiple_of(i * 8, 8), 8)
        cell = cell_ref[here, :]
        code = code_ref[here, :]
        slot = (((code >> 5) & 3) << 3) | ((code >> 7) & 7)
        group = code & 31
        mass = buf_ref[6, here, :]
        vals = [buf_ref[c, here, :] - 0.5 * TG for c in range(3)] + [mass]
        for c in range(3):
            v = buf_ref[3 + c, here, :]
            vel_ref[c, here, :] = v
            vals.append(mass * v)
        high_part = [v.astype(BF16).astype(F32) for v in vals]
        low_part = [v - h for v, h in zip(vals, high_part)]
        slot_f, group_f = slot.astype(F32), group.astype(F32)

        def spread(v, r):
            return jnp.broadcast_to(v[r:r + 1], (32, LANES)).astype(BF16)

        for r in range(8):
            lanes = slice(r * LANES, (r + 1) * LANES)
            at_group = iota_b == spread(group_f, r)
            at_slot = iota_b == spread(slot_f, r)
            cell_r = spread(cell, r)
            hot = jnp.where(at_group, one_b, zero_b)
            for d in range(27):
                lhs[d * 32:(d + 1) * 32, lanes] = jnp.where(cell_r == jnp.asarray(d, BF16), hot, zero_b)
            lhs2[:, lanes] = jnp.where(iota_b == cell_r, one_b, zero_b)
            for half, parts in ((0, high_part), (1, low_part)):
                for c in range(4):
                    o = half * 128 + c * 32
                    rhs[o:o + 32, lanes] = jnp.where(at_slot, spread(parts[c], r), zero_b)
                for c in range(3):
                    o = half * 96 + c * 32
                    rhs2[o:o + 32, lanes] = jnp.where(at_group, spread(parts[4 + c], r), zero_b)

    def add(lhs, rhs, lhs2, rhs2):
        acc_ref[...] += lax.dot_general(lhs[...], rhs[...], NT, preferred_element_type=F32)
        acc2_ref[0:32, :] += lax.dot_general(lhs2[...], rhs2[...], NT, preferred_element_type=F32)

    slot_a = (lhs_a, rhs_a, lhs2_a, rhs2_a)
    slot_b = (lhs_b, rhs_b, lhs2_b, rhs2_b)
    build(0, *slot_a)

    def scatter(i, carry):
        build(2 * i + 1, *slot_b)
        add(*slot_a)
        build(2 * i + 2, *slot_a)
        add(*slot_b)
        return carry

    lax.fori_loop(0, (n_blocks + 1) // 2, scatter, 0)
    for a, out in enumerate((out_m, out_0, out_p)):
        out[0:288, :] = acc_ref[a * 288:(a + 1) * 288, 0:128] + acc_ref[a * 288:(a + 1) * 288, 128:256]
        for b in range(3):
            at = slice(MEMBER_ROWS + 8 * b, MEMBER_ROWS + 8 * b + 8)
            first = a * 9 + b * 3
            mom = acc2_ref[first:first + 8, 0:96] + acc2_ref[first:first + 8, 96:192]
            out[at, :] = jnp.concatenate([mom, jnp.zeros((8, 32), F32)], axis=1)


def members(coords, counts, table, parts):
    rows = parts.shape[1]
    send = (TOP_X + 4 * TG * TG, LANES)

    def kernel(coords_ref, *rest):
        member_kernel(counts, [coords_ref[k] for k in range(3)], *rest)

    shapes = [(send, F32), ((TOP_X, LANES), F32), (send, F32), ((4, 4 * TG * TG, LANES), F32), ((rows, LANES), I32),
              ((rows + PAD, LANES), I32), ((3, rows + PAD, LANES), F32), ((1,), I32)]
    specs = [pl.BlockSpec(memory_space=VMEM)] * 8
    specs[7] = pl.BlockSpec(memory_space=pltpu.SMEM)
    return pl.pallas_call(
        kernel,
        out_shape=[jax.ShapeDtypeStruct(s, d) for s, d in shapes],
        in_specs=[pl.BlockSpec(memory_space=m) for m in [pltpu.SMEM] + [pltpu.HBM] * 2],
        out_specs=specs,
        scratch_shapes=[
            VMEM((rows + 256, LANES), I32),
            VMEM((7, rows + 256, LANES), F32),
            VMEM(table.shape, I32),
            VMEM((rows + PAD, LANES), F32),
        ] + [VMEM((27 * 32, 1024), BF16)] * 2 + [VMEM((256, 1024), BF16)] * 2
        + [VMEM((32, 1024), BF16)] * 2 + [VMEM((192, 1024), BF16)] * 2 + [
            VMEM((27 * 32, 256), F32),
            VMEM((40, 192), F32),
            pltpu.SemaphoreType.DMA((2,)),
        ],
        compiler_params=pltpu.CompilerParams(vmem_limit_bytes=VMEM_LIMIT),
    )(coords, table, parts)


def inverse_distance(target, source):
    dx = target[0] - source[0]
    dy = target[1] - source[1]
    dz = target[2] - source[2]
    return lax.rsqrt(dx * dx + dy * dy + (dz * dz + SOFTENING))


def sym_pairs(target, acc, source, base, first, offsets, once=(), skip_self=False, lone=()):
    src = [[row(ref, base + first + r) for ref in source] for r in range(4)]
    gains = [jnp.zeros((8, LANES), F32) for _ in range(4)]
    sublane = lax.broadcasted_iota(I32, (8, LANES), 0)
    for t in list(offsets) + list(lone):
        at = pl.ds(pl.multiple_of(base + 8 * t, 8), 8)
        tgt = [ref[at, :] for ref in target]
        total = acc[at, :]
        for r in range(4):
            inv = inverse_distance(tgt, src[r])
            mine = inv * src[r][3]
            if skip_self and t == 0:
                mine = jnp.where(sublane == first + r, 0.0, mine)
            total = total + mine
            if t in offsets:
                gains[r] = gains[r] + inv * tgt[3]
        acc[at, :] = total
    return [jnp.sum(g, axis=0, keepdims=True) for g in gains]


def near_kernel(axes, parts_ref, out_ref, xs, ys, zs, ms, acc):
    target = (xs, ys, zs, ms)
    tiles = 2 * TG * TG
    for k, axis in enumerate(axes):
        for ref, c in zip(target, (0, 1, 2, 6)):
            t = jnp.transpose(parts_ref[c, axis * tiles:(axis + 1) * tiles, :])
            ref[0:128, :] = t
            ref[128:256, :] = t
        acc[...] = jnp.zeros_like(acc)

        def body(jb, carry):
            base = pl.multiple_of(jb * 8, 8)
            for first in (0, 4):
                gains = sym_pairs(target, acc, target, base, first, range(1, 8), skip_self=True, lone=(0, 8))
                for r in range(4):
                    at = pl.ds(base + first + r, 1)
                    acc[at, :] = acc[at, :] + gains[r]
            return carry

        lax.fori_loop(0, 16, body, 0)
        out_ref[k * 128:(k + 1) * 128, :] = acc[0:128, :] + acc[128:256, :]


def far_kernel(axis, n_done, parts_ref, near_ref, low_ref, high_ref, *rest):
    done, (out_ref, xs, ys, zs, ms, acc) = rest[:n_done], rest[n_done:]
    for k, ref in enumerate(done):
        out_ref[k * 128:(k + 1) * 128, :] = ref[...]
    tiles = TG * TG
    source = (xs, ys, zs, ms)
    target = []
    for k, (ref, c) in enumerate(zip(source, (0, 1, 2, 6))):
        low = low_ref[k * tiles:(k + 1) * tiles, :]
        high = high_ref[k * tiles:(k + 1) * tiles, :]
        if k == axis:
            low = low - 1.0 * TG
            high = high + 1.0 * TG
        ref[...] = jnp.transpose(jnp.concatenate([low, high], axis=0))
    tgt_refs = acc
    for k, c in enumerate((0, 1, 2)):
        tgt_refs[k, :, :] = jnp.transpose(parts_ref[c, axis * 2 * tiles:(axis + 1) * 2 * tiles, :])
    tgt_refs[3, :, :] = near_ref[...]

    def body(jb, carry):
        base = pl.multiple_of(jb * 4, 4)
        src = [[row(ref, base + r) for ref in source] for r in range(4)]
        for t in range(16):
            at = slice(8 * t, 8 * t + 8)
            tgt = [tgt_refs[k, at, :] for k in range(3)]
            total = tgt_refs[3, at, :]
            for r in range(4):
                total = total + inverse_distance(tgt, src[r]) * src[r][3]
            tgt_refs[3, at, :] = total
        return carry

    lax.fori_loop(0, 32, body, 0)
    out_ref[n_done * 128:(n_done + 1) * 128, :] = jnp.transpose(tgt_refs[3, :, :]) * (-EDGE_COUPLING)


def near(axes, parts, after):
    return call(functools.partial(near_kernel, axes), [((128 * len(axes), LANES), F32)], 1,
                [VMEM((256, LANES), F32)] * 5, after=after)(parts)[0]


def far(axis, parts, near_part, low, high, after=(), done=()):
    return call(functools.partial(far_kernel, axis, len(done)), [((128 * (len(done) + 1), LANES), F32)],
                4 + len(done), [VMEM((128, LANES), F32)] * 4 + [VMEM((4, 128, LANES), F32)], after=after)(
                    parts, near_part, low, high, *done)[0]


def group_kernel(low_ref, mid_ref, high_ref, out_m, out_0, out_p,
                 x0, y0, z0, m0, acc, s1, s2, g1, g2):
    base = (x0, y0, z0, m0)
    n_rows = 27 * 8
    quarter = lax.broadcasted_iota(I32, (8, LANES), 1) // 32
    received = (low_ref, mid_ref, high_ref)
    mom = jnp.zeros((8, LANES), F32)
    cells = []
    for e in range(28):
        if e == 27:
            cells.append(jnp.zeros((32, LANES), F32))
        else:
            ref, within = received[e // 9], e % 9
            cells.append(ref[within * 32:within * 32 + 32, :])
    for ref, dz in zip(received, (2, 1, 0)):
        mom = mom + jnp.broadcast_to(ref[MEMBER_ROWS + dz:MEMBER_ROWS + dz + 1, :], (8, LANES))
    for blk in range(7):
        flat = jnp.transpose(jnp.concatenate(cells[blk * 4:blk * 4 + 4], axis=0))
        for c in range(4):
            quads = [flat[c * 32 + q * 8:c * 32 + q * 8 + 8, :] for q in range(4)]
            for a in range(4):
                e = blk * 4 + a
                if e == 27:
                    continue
                mixed = None
                for q in range(4):
                    moved = quads[q] if q == a else pltpu.roll(quads[q], (32 * (q - a)) % 128, 1)
                    mixed = moved if mixed is None else jnp.where(quarter == q, moved, mixed)
                if c < 3:
                    d = (e % 3, e // 3 % 3, e // 9)[c] - 1
                    mixed = mixed + float(TG * d)
                base[c][e * 8:e * 8 + 8, :] = mixed
                base[c][n_rows + e * 8:n_rows + e * 8 + 8, :] = mixed
    for c in range(4):
        v = base[c][0:n_rows, :]
        s1[c, :, :] = pltpu.roll(v, 96, 1)
        s2[c, :, :] = pltpu.roll(v, 64, 1)
    acc[...] = jnp.zeros_like(acc)
    src1 = tuple(s1.at[c] for c in range(4))
    src2 = tuple(s2.at[c] for c in range(4))

    def body(jb, carry):
        at0 = pl.multiple_of(jb * 8, 8)
        for first in (0, 4):
            own = sym_pairs(base, acc, base, at0, first, range(1, 14), skip_self=True, lone=(0,))
            one = sym_pairs(base, acc, src1, at0, first, range(0, 27))
            two = sym_pairs(base, acc, src2, at0, first, range(1, 14), lone=(0,))
            for r in range(4):
                at = pl.ds(at0 + first + r, 1)
                acc[at, :] = acc[at, :] + own[r]
                g1[at, :] = one[r]
                g2[at, :] = two[r]
        return carry

    lax.fori_loop(0, 27, body, 0)
    total = (acc[0:n_rows, :] + acc[n_rows:2 * n_rows, :]
             + pltpu.roll(g1[...], 32, 1) + pltpu.roll(g2[...], 64, 1))
    mass = jnp.sum(m0[0:n_rows, :], axis=0, keepdims=True)
    mass = jnp.broadcast_to(mass, (8, LANES))
    mass = mass + pltpu.roll(mass, 32, 1)
    mass = mass + pltpu.roll(mass, 64, 1)
    mean = mom / mass
    for zs, out in enumerate((out_m, out_0, out_p)):
        out[0:72, :] = total[zs * 72:(zs + 1) * 72, :] * (-GROUP_COUPLING)
        out[72:80, :] = mean


def groups(low, mid, high, after):
    rows = 27 * 8
    return call(group_kernel, [((80, LANES), F32)] * 3, 3,
                [VMEM((2 * rows, LANES), F32)] * 5 + [VMEM((4, rows, LANES), F32)] * 2
                + [VMEM((rows, LANES), F32)] * 2, after=after)(low, mid, high)


def energy_kernel(blocks_ref, low_ref, mid_ref, high_ref, code_ref, vel_ref, bits_ref, keys_ref, out_ref,
                  buf_ref, pot_ref, mean_ref, table_ref, hot_a, hot_b, got_a, got_b):
    received = (low_ref, mid_ref, high_ref)
    rows = bits_ref.shape[0]
    pot_ref[216:256, :] = jnp.zeros((40, LANES), F32)
    mean_ref[216:256, :] = jnp.zeros((40, LANES), F32)
    for cell in range(27):
        ref, within = received[cell // 9], cell % 9
        pot_ref[cell * 8:cell * 8 + 8, :] = ref[within * 16:within * 16 + 8, :]
        mean_ref[cell * 8:cell * 8 + 8, :] = ref[within * 16 + 8:within * 16 + 16, :]
    for k, ref in enumerate((pot_ref, mean_ref)):
        for half in range(2):
            lanes = slice(half * LANES, (half + 1) * LANES)
            flipped = jnp.transpose(ref[lanes, :])
            high = flipped.astype(BF16)
            low = (flipped - high.astype(F32)).astype(BF16)
            base, size = ((0, 128), (256, 96))[k]
            table_ref[base:base + size, lanes] = high[0:size]
            table_ref[base + size:base + 2 * size, lanes] = low[0:size]
    iota_row = lax.broadcasted_iota(I32, (224, LANES), 0).astype(F32).astype(BF16)
    iota_lane = lax.broadcasted_iota(I32, (LANES, LANES), 0)
    iota_group = lax.broadcasted_iota(I32, (32, LANES), 0)
    one_b, zero_b = jnp.ones((224, LANES), BF16), jnp.zeros((224, LANES), BF16)
    hot_a[224:256, :] = jnp.zeros((32, 1024), BF16)
    hot_b[224:256, :] = jnp.zeros((32, 1024), BF16)

    def mark(i, hot_ref):
        at_row = (code_ref[pl.ds(pl.multiple_of(i * 8, 8), 8), :] >> 7).astype(F32)
        for r in range(8):
            lanes = slice(r * LANES, (r + 1) * LANES)
            want = jnp.broadcast_to(at_row[r:r + 1], (224, LANES)).astype(BF16)
            hot_ref[0:224, lanes] = jnp.where(iota_row == want, one_b, zero_b)

    def fetch(i, hot_ref, got_ref):
        here = pl.ds(pl.multiple_of(i * 8, 8), 8)
        code = code_ref[here, :]
        lane = code & 127
        group = code & 31
        for pair in range(4):
            found = jnp.dot(table_ref[...], hot_ref[:, pair * 256:(pair + 1) * 256], preferred_element_type=F32)
            for k in range(2):
                r = pair * 2 + k
                lanes = slice(k * LANES, (k + 1) * LANES)
                pot = found[0:128, lanes] + found[128:256, lanes]
                pot = jnp.where(iota_lane == jnp.broadcast_to(lane[r:r + 1], (LANES, LANES)), pot, 0.0)
                got_ref[0, r:r + 1, :] = jnp.sum(pot, axis=0, keepdims=True)
                at_group = iota_group == jnp.broadcast_to(group[r:r + 1], (32, LANES))
                for c in range(3):
                    o = 256 + c * 32
                    mean = found[o:o + 32, lanes] + found[o + 96:o + 128, lanes]
                    got_ref[1 + c, r:r + 1, :] = jnp.sum(jnp.where(at_group, mean, 0.0), axis=0, keepdims=True)
        kinetic = jnp.zeros((8, LANES), F32)
        for c in range(3):
            diff = vel_ref[c, here, :] - got_ref[1 + c]
            kinetic = kinetic + diff * diff
        buf_ref[pl.ds(pl.multiple_of(i * 8 + 256, 8), 8), :] = got_ref[0] + 0.5 * kinetic

    mark(0, hot_a)

    def gather(i, carry):
        mark(2 * i + 1, hot_b)
        fetch(2 * i, hot_a, got_a)
        mark(2 * i + 2, hot_a)
        fetch(2 * i + 1, hot_b, got_b)
        return carry

    lax.fori_loop(0, (blocks_ref[0] + 1) // 2, gather, 0)
    step_rows = 32
    for stage in reversed(range(STAGES)):
        d = 1 << stage

        def move(i, carry, d=d):
            base = pl.multiple_of((rows // step_rows - 1 - i) * step_rows, step_rows)
            moved = (bits_ref[pl.ds(base, step_rows), :] & d) != 0
            here = pl.ds(pl.multiple_of(base + 256, 8), step_rows)
            buf_ref[here, :] = jnp.where(moved, buf_ref[pl.ds(base + 256 - d, step_rows), :], buf_ref[here, :])
            return carry

        lax.fori_loop(0, rows // step_rows, move, 0)
    out_ref[...] = jnp.where(keys_ref[0:rows, :] < (keys_ref.shape[0] - rows) * LANES * GCAP, buf_ref[pl.ds(256, rows), :], 0.0)


def energies(blocks, low, mid, high, code, vel, bits, table):
    rows = bits.shape[0]
    scratch = [VMEM((rows + 256, LANES), F32), VMEM((256, LANES), F32), VMEM((256, LANES), F32),
               VMEM((448, 256), BF16)] + [VMEM((256, 1024), BF16)] * 2 + [VMEM((4, 8, LANES), F32)] * 2
    return call(energy_kernel, [((rows, LANES), F32)], 8, scratch, smem_first=True)(
        blocks, low, mid, high, code, vel, bits, table)[0]


def up(axis, x):
    n = lax.axis_size(axis)
    return lax.ppermute(x, axis, [(i, (i + 1) % n) for i in range(n)])


def down(axis, x):
    n = lax.axis_size(axis)
    return lax.ppermute(x, axis, [((i + 1) % n, i) for i in range(n)])


def local(particles, labels, member_slot, owner_slot):
    slab_all = particles.shape[-1]
    rows = slab_all // LANES
    parts = particles.reshape(7, rows, LANES)
    keys = labels.reshape(rows, LANES) * GCAP + member_slot.reshape(rows, LANES)
    table = jnp.concatenate([keys, owner_slot.reshape(-1, LANES)], axis=0)
    counts = tuple(lax.axis_size(a) for a in ("gx", "gy", "gz"))
    coords = jnp.stack([lax.axis_index(a) for a in ("gx", "gy", "gz")]).astype(I32)
    send_m, keep, send_p, faces, bits, code, vel, n_blocks = members(coords, counts, table, parts)
    from_low = up("gx", send_p)
    from_high = down("gx", send_m)
    ghost_low = up("gz", faces[3])
    ghost_high = down("gz", faces[2])
    near_xy = near((0, 1), parts, (keep,))
    x_all = (from_low, keep, from_high)

    sums = lax.broadcasted_iota(I32, (8, LANES), 0) < 3

    def stack_y(b):
        mom = sum(t[MEMBER_ROWS + 8 * b:MEMBER_ROWS + 8 * b + 8] for t in x_all)
        return [t[b * 96:(b + 1) * 96] for t in x_all] + [jnp.where(sums, mom, near_xy[0:8])]

    y_low = up("gy", jnp.concatenate(stack_y(2) + [faces[1]], axis=0))
    y_high = down("gy", jnp.concatenate(stack_y(0) + [faces[0]], axis=0))
    y_keep = jnp.concatenate(stack_y(1), axis=0)
    near_z = near((2,), parts, (y_keep,))
    edge_x = far(0, parts, near_xy[0:128], from_low[TOP_X:], from_high[TOP_X:], (y_keep,))
    y_all = (y_low, y_keep, y_high)
    mom_z = sum(t[MEMBER_ROWS:TOP] for t in y_all)
    mom_z = jnp.where(sums, mom_z, edge_x[0:8] + near_z[0:8])

    def stack_z(b):
        return [t[(3 * xs + b) * 32:(3 * xs + b + 1) * 32] for t in y_all for xs in range(3)] + [mom_z]

    z_low = up("gz", jnp.concatenate(stack_z(2), axis=0))
    z_high = down("gz", jnp.concatenate(stack_z(0), axis=0))
    z_keep = jnp.concatenate(stack_z(1), axis=0)
    edge_y = far(1, parts, near_xy[128:256], y_low[TOP:], y_high[TOP:], (z_keep,))
    to_low, stay, to_high = groups(z_low, z_keep, z_high, (edge_y,))
    edge = far(2, parts, near_z, ghost_low, ghost_high, (stay,), (edge_x, edge_y))
    back_high = down("gz", to_low)
    back_low = up("gz", to_high)
    zs = (back_low, stay, back_high)

    def back_y(b):
        return jnp.concatenate([p for t in zs for p in (t[b * 24:(b + 1) * 24], t[72:80])], axis=0)

    ylow = up("gy", back_y(2))
    yhigh = down("gy", back_y(0))
    ys = (ylow, back_y(1), yhigh)

    def back_x(b):
        return jnp.concatenate(
            [p for z in range(3) for t in ys
             for p in (t[z * 32 + b * 8:z * 32 + b * 8 + 8], t[z * 32 + 24:z * 32 + 32])], axis=0)

    xlow = up("gx", back_x(2))
    xhigh = down("gx", back_x(0))
    energy = energies(n_blocks, xlow, back_x(1), xhigh, code, vel, bits, table)
    return edge.reshape(1, 1, 1, slab_all), energy.reshape(1, 1, 1, slab_all)


def solution(mesh):
    return jax.shard_map(
        local,
        mesh=mesh,
        in_specs=(
            P(None, "gx", "gy", "gz", None),
            P("gx", "gy", "gz", None),
            P("gx", "gy", "gz", None),
            P(),
        ),
        out_specs=(P("gx", "gy", "gz", None), P("gx", "gy", "gz", None)),
        check_vma=False,
    )
```

```python
import functools

import jax
import jax.numpy as jnp
from jax import lax
from jax.experimental import pallas as pl
from jax.experimental.pallas import tpu as pltpu
from jax.sharding import PartitionSpec as P

TG = 8
GCAP = 32
LANES = 128
SOFTENING = 0.01
EDGE_COUPLING = 1.0 / 256.0
GROUP_COUPLING = 1.0 / 16.0
VMEM_LIMIT = 32 * 1024 * 1024
MEMBER_ROWS = 9 * 32
TOP = MEMBER_ROWS + 8
TOP_X = MEMBER_ROWS + 24
VMEM = pltpu.VMEM
F32 = jnp.float32
BF16 = jnp.bfloat16
I32 = jnp.int32


def call(kernel, outs, n_in, scratch, smem_first=False, after=()):
    after = tuple(a[0:8] for a in after)
    specs = [pl.BlockSpec(memory_space=VMEM)] * n_in + [pl.BlockSpec(memory_space=VMEM)] * len(after)
    if smem_first:
        specs[0] = pl.BlockSpec(memory_space=pltpu.SMEM)

    def body(*refs):
        kernel(*refs[:n_in], *refs[n_in + len(after):])

    run = pl.pallas_call(
        body,
        out_shape=[jax.ShapeDtypeStruct(s, d) for s, d in outs],
        in_specs=specs,
        out_specs=[pl.BlockSpec(memory_space=VMEM)] * len(outs),
        scratch_shapes=scratch,
        compiler_params=pltpu.CompilerParams(vmem_limit_bytes=VMEM_LIMIT),
    )
    return lambda *args: run(*args, *after)


def row(ref, index):
    return jnp.broadcast_to(ref[pl.ds(index, 1), :], (8, LANES))


def take_lanes(values, index):
    return jnp.take_along_axis(values, index, axis=1, mode="promise_in_bounds")


STAGES = 9
INVALID = (4096 * 32) << STAGES
PAD = 16
NT = (((1,), (1,)), ((), ()))


def owner_offset(mine, theirs, n):
    if n & (n - 1):
        step = (mine - theirs + n // 2 + n) % n - n // 2
    else:
        step = ((mine - theirs + n // 2) & (n - 1)) - n // 2
    return 1 - step


def member_kernel(counts, coords, table_hbm, parts_hbm,
                  out_m, out_0, out_p, faces_ref, bits_ref, code_ref, vel_ref, blocks_ref,
                  word_ref, buf_ref, table_ref, cell_ref, lhs_a, lhs_b, rhs_a, rhs_b,
                  lhs2_a, lhs2_b, rhs2_a, rhs2_b, acc_ref, acc2_ref, sems):
    rows = parts_hbm.shape[1]
    owner_ref = table_ref.at[pl.ds(rows, table_ref.shape[0] - rows), :]
    ngroups = owner_ref.shape[0] * LANES
    copies = [
        pltpu.make_async_copy(table_hbm, table_ref, sems.at[0]),
        pltpu.make_async_copy(parts_hbm, buf_ref.at[:, pl.ds(0, rows), :], sems.at[1]),
    ]
    for copy in copies:
        copy.start()
    word_ref[pl.ds(rows, 256), :] = jnp.full((256, LANES), INVALID, I32)
    acc_ref[...] = jnp.zeros_like(acc_ref)
    acc2_ref[...] = jnp.zeros_like(acc2_ref)
    bits_ref[...] = jnp.zeros_like(bits_ref)
    for c in range(7):
        buf_ref[c, pl.ds(rows, PAD), :] = jnp.zeros((PAD, LANES), F32)
    below = lax.broadcasted_iota(I32, (rows, rows), 0) > lax.broadcasted_iota(I32, (rows, rows), 1)
    below = jnp.where(below, 1.0, 0.0).astype(BF16)
    copies[0].wait()
    keys = table_ref[0:rows, :]
    member = keys < ngroups * GCAP
    flags = jnp.where(member, 1.0, 0.0)
    rank = jnp.dot(below, flags.astype(BF16), preferred_element_type=F32)
    place = lax.broadcasted_iota(I32, (rows, LANES), 0)
    shift = place - rank.astype(I32)
    word = (keys << STAGES) | shift
    word_ref[pl.ds(0, rows), :] = jnp.where(member, word, INVALID)
    tops = jnp.max(rank + flags, axis=0, keepdims=True)
    n_blocks = (jnp.max(tops).astype(I32) + 7) // 8
    blocks_ref[0] = n_blocks
    copies[1].wait()
    tiles = TG * TG
    for out, face in ((out_m, 0), (out_p, 1)):
        for k, c in enumerate((0, 1, 2, 6)):
            out[TOP_X + k * tiles:TOP_X + (k + 1) * tiles, :] = buf_ref[c, face * tiles:(face + 1) * tiles, :]
    for face in range(2, 6):
        for k, c in enumerate((0, 1, 2, 6)):
            faces_ref[face - 2, k * tiles:(k + 1) * tiles, :] = buf_ref[c, face * tiles:(face + 1) * tiles, :]
    step_rows = 32
    for stage in range(STAGES):
        d = 1 << stage

        def move(i, carry, d=d):
            base = pl.multiple_of(i * step_rows, step_rows)
            here = pl.ds(base, step_rows)
            there = pl.ds(base + d, step_rows)
            own = word_ref[here, :]
            far = word_ref[there, :]
            bits_ref[here, :] = bits_ref[here, :] | (own & d)
            comes = (far & d) != 0
            goes = (own & d) != 0
            word_ref[here, :] = jnp.where(comes, far, jnp.where(goes, INVALID, own))
            for c in range(7):
                buf_ref[c, here, :] = jnp.where(comes, buf_ref[c, there, :], buf_ref[c, here, :])
            return carry

        lax.fori_loop(0, rows // step_rows, move, 0)

    iota32 = lax.broadcasted_iota(I32, (32, LANES), 0)
    iota_b = iota32.astype(F32).astype(BF16)
    zero_b = jnp.zeros((32, LANES), BF16)
    one_b = jnp.ones((32, LANES), BF16)

    def decode(i, carry):
        here = pl.ds(pl.multiple_of(i * PAD, PAD), PAD)
        key = word_ref[here, :] >> STAGES
        valid = key < ngroups * GCAP
        lab = key >> 5
        slot = key & 31
        low = lab & 127
        high = lab >> 7
        owner = jnp.zeros((PAD, LANES), I32)
        for r in range(ngroups // LANES):
            found = take_lanes(jnp.broadcast_to(owner_ref[pl.ds(r, 1), :], (PAD, LANES)), low)
            owner = jnp.where(high == r, found, owner)
        group = owner & 31
        device = owner >> 5
        nx, ny, nz = counts
        ox = owner_offset(coords[0], device // (nz * ny), nx)
        oy = owner_offset(coords[1], device // nz % ny, ny)
        oz = owner_offset(coords[2], device % nz, nz)
        cell_ref[here, :] = jnp.where(valid, (ox * 3 + oy) * 3 + oz, -1).astype(F32)
        code = (((ox * 9 + oz * 3 + oy) * 8 + (slot & 7)) << 7) | ((slot >> 3) << 5) | group
        code_ref[here, :] = jnp.where(valid, code, 0)
        return carry

    lax.fori_loop(0, jnp.minimum((n_blocks + 4) // 2, (rows + PAD) // PAD), decode, 0)

    def build(i, lhs, rhs, lhs2, rhs2):
        here = pl.ds(pl.multiple_of(i * 8, 8), 8)
        cell = cell_ref[here, :]
        code = code_ref[here, :]
        slot = (((code >> 5) & 3) << 3) | ((code >> 7) & 7)
        group = code & 31
        mass = buf_ref[6, here, :]
        vals = [buf_ref[c, here, :] - 0.5 * TG for c in range(3)] + [mass]
        for c in range(3):
            v = buf_ref[3 + c, here, :]
            vel_ref[c, here, :] = v
            vals.append(mass * v)
        high_part = [v.astype(BF16).astype(F32) for v in vals]
        low_part = [v - h for v, h in zip(vals, high_part)]
        slot_f, group_f = slot.astype(F32), group.astype(F32)

        def spread(v, r):
            return jnp.broadcast_to(v[r:r + 1], (32, LANES)).astype(BF16)

        for r in range(8):
            lanes = slice(r * LANES, (r + 1) * LANES)
            at_group = iota_b == spread(group_f, r)
            at_slot = iota_b == spread(slot_f, r)
            cell_r = spread(cell, r)
            hot = jnp.where(at_group, one_b, zero_b)
            for d in range(27):
                lhs[d * 32:(d + 1) * 32, lanes] = jnp.where(cell_r == jnp.asarray(d, BF16), hot, zero_b)
            lhs2[:, lanes] = jnp.where(iota_b == cell_r, one_b, zero_b)
            for half, parts in ((0, high_part), (1, low_part)):
                for c in range(4):
                    o = half * 128 + c * 32
                    rhs[o:o + 32, lanes] = jnp.where(at_slot, spread(parts[c], r), zero_b)
                for c in range(3):
                    o = half * 96 + c * 32
                    rhs2[o:o + 32, lanes] = jnp.where(at_group, spread(parts[4 + c], r), zero_b)

    def add(lhs, rhs, lhs2, rhs2):
        acc_ref[...] += lax.dot_general(lhs[...], rhs[...], NT, preferred_element_type=F32)
        acc2_ref[0:32, :] += lax.dot_general(lhs2[...], rhs2[...], NT, preferred_element_type=F32)

    slot_a = (lhs_a, rhs_a, lhs2_a, rhs2_a)
    slot_b = (lhs_b, rhs_b, lhs2_b, rhs2_b)
    build(0, *slot_a)

    def scatter(i, carry):
        build(2 * i + 1, *slot_b)
        add(*slot_a)
        build(2 * i + 2, *slot_a)
        add(*slot_b)
        return carry

    lax.fori_loop(0, (n_blocks + 1) // 2, scatter, 0)
    for a, out in enumerate((out_m, out_0, out_p)):
        out[0:288, :] = acc_ref[a * 288:(a + 1) * 288, 0:128] + acc_ref[a * 288:(a + 1) * 288, 128:256]
        for b in range(3):
            at = slice(MEMBER_ROWS + 8 * b, MEMBER_ROWS + 8 * b + 8)
            first = a * 9 + b * 3
            mom = acc2_ref[first:first + 8, 0:96] + acc2_ref[first:first + 8, 96:192]
            out[at, :] = jnp.concatenate([mom, jnp.zeros((8, 32), F32)], axis=1)


def members(coords, counts, table, parts):
    rows = parts.shape[1]
    send = (TOP_X + 4 * TG * TG, LANES)

    def kernel(coords_ref, *rest):
        member_kernel(counts, [coords_ref[k] for k in range(3)], *rest)

    shapes = [(send, F32), ((TOP_X, LANES), F32), (send, F32), ((4, 4 * TG * TG, LANES), F32), ((rows, LANES), I32),
              ((rows + PAD, LANES), I32), ((3, rows + PAD, LANES), F32), ((1,), I32)]
    specs = [pl.BlockSpec(memory_space=VMEM)] * 8
    specs[7] = pl.BlockSpec(memory_space=pltpu.SMEM)
    return pl.pallas_call(
        kernel,
        out_shape=[jax.ShapeDtypeStruct(s, d) for s, d in shapes],
        in_specs=[pl.BlockSpec(memory_space=m) for m in [pltpu.SMEM] + [pltpu.HBM] * 2],
        out_specs=specs,
        scratch_shapes=[
            VMEM((rows + 256, LANES), I32),
            VMEM((7, rows + 256, LANES), F32),
            VMEM(table.shape, I32),
            VMEM((rows + PAD, LANES), F32),
        ] + [VMEM((27 * 32, 1024), BF16)] * 2 + [VMEM((256, 1024), BF16)] * 2
        + [VMEM((32, 1024), BF16)] * 2 + [VMEM((192, 1024), BF16)] * 2 + [
            VMEM((27 * 32, 256), F32),
            VMEM((40, 192), F32),
            pltpu.SemaphoreType.DMA((2,)),
        ],
        compiler_params=pltpu.CompilerParams(vmem_limit_bytes=VMEM_LIMIT),
    )(coords, table, parts)


def inverse_distance(target, source):
    dx = target[0] - source[0]
    dy = target[1] - source[1]
    dz = target[2] - source[2]
    return lax.rsqrt(dx * dx + dy * dy + (dz * dz + SOFTENING))


def sym_pairs(target, acc, source, base, first, offsets, once=(), skip_self=False, lone=()):
    src = [[row(ref, base + first + r) for ref in source] for r in range(4)]
    gains = [jnp.zeros((8, LANES), F32) for _ in range(4)]
    sublane = lax.broadcasted_iota(I32, (8, LANES), 0)
    for t in list(offsets) + list(lone):
        at = pl.ds(pl.multiple_of(base + 8 * t, 8), 8)
        tgt = [ref[at, :] for ref in target]
        total = acc[at, :]
        for r in range(4):
            inv = inverse_distance(tgt, src[r])
            mine = inv * src[r][3]
            if skip_self and t == 0:
                mine = jnp.where(sublane == first + r, 0.0, mine)
            total = total + mine
            if t in offsets:
                gains[r] = gains[r] + inv * tgt[3]
        acc[at, :] = total
    return [jnp.sum(g, axis=0, keepdims=True) for g in gains]


def near_kernel(axes, parts_ref, out_ref, xs, ys, zs, ms, acc):
    target = (xs, ys, zs, ms)
    tiles = 2 * TG * TG
    for k, axis in enumerate(axes):
        for ref, c in zip(target, (0, 1, 2, 6)):
            t = jnp.transpose(parts_ref[c, axis * tiles:(axis + 1) * tiles, :])
            ref[0:128, :] = t
            ref[128:256, :] = t
        acc[...] = jnp.zeros_like(acc)

        def body(jb, carry):
            base = pl.multiple_of(jb * 8, 8)
            for first in (0, 4):
                gains = sym_pairs(target, acc, target, base, first, range(1, 8), skip_self=True, lone=(0, 8))
                for r in range(4):
                    at = pl.ds(base + first + r, 1)
                    acc[at, :] = acc[at, :] + gains[r]
            return carry

        lax.fori_loop(0, 16, body, 0)
        out_ref[k * 128:(k + 1) * 128, :] = acc[0:128, :] + acc[128:256, :]


def far_kernel(axis, n_done, parts_ref, near_ref, low_ref, high_ref, *rest):
    done, (out_ref, xs, ys, zs, ms, acc) = rest[:n_done], rest[n_done:]
    for k, ref in zip([k for k in range(3) if k != axis], done):
        out_ref[k * 128:(k + 1) * 128, :] = ref[...]
    tiles = TG * TG
    source = (xs, ys, zs, ms)
    target = []
    for k, (ref, c) in enumerate(zip(source, (0, 1, 2, 6))):
        low = low_ref[k * tiles:(k + 1) * tiles, :]
        high = high_ref[k * tiles:(k + 1) * tiles, :]
        if k == axis:
            low = low - 1.0 * TG
            high = high + 1.0 * TG
        ref[...] = jnp.transpose(jnp.concatenate([low, high], axis=0))
    tgt_refs = acc
    for k, c in enumerate((0, 1, 2)):
        tgt_refs[k, :, :] = jnp.transpose(parts_ref[c, axis * 2 * tiles:(axis + 1) * 2 * tiles, :])
    tgt_refs[3, :, :] = near_ref[...]

    def body(jb, carry):
        base = pl.multiple_of(jb * 4, 4)
        src = [[row(ref, base + r) for ref in source] for r in range(4)]
        for t in range(16):
            at = slice(8 * t, 8 * t + 8)
            tgt = [tgt_refs[k, at, :] for k in range(3)]
            total = tgt_refs[3, at, :]
            for r in range(4):
                total = total + inverse_distance(tgt, src[r]) * src[r][3]
            tgt_refs[3, at, :] = total
        return carry

    lax.fori_loop(0, 32, body, 0)
    mine = axis if n_done else 0
    out_ref[mine * 128:(mine + 1) * 128, :] = jnp.transpose(tgt_refs[3, :, :]) * (-EDGE_COUPLING)


def near(axes, parts, after):
    return call(functools.partial(near_kernel, axes), [((128 * len(axes), LANES), F32)], 1,
                [VMEM((256, LANES), F32)] * 5, after=after)(parts)[0]


def far(axis, parts, near_part, low, high, after=(), done=()):
    return call(functools.partial(far_kernel, axis, len(done)), [((128 * (len(done) + 1), LANES), F32)],
                4 + len(done), [VMEM((128, LANES), F32)] * 4 + [VMEM((4, 128, LANES), F32)], after=after)(
                    parts, near_part, low, high, *done)[0]


def group_kernel(low_ref, mid_ref, high_ref, out_m, out_0, out_p,
                 x0, y0, z0, m0, acc, s1, s2, g1, g2):
    base = (x0, y0, z0, m0)
    n_rows = 27 * 8
    quarter = lax.broadcasted_iota(I32, (8, LANES), 1) // 32
    received = (low_ref, mid_ref, high_ref)
    mom = jnp.zeros((8, LANES), F32)
    cells = []
    for e in range(28):
        if e == 27:
            cells.append(jnp.zeros((32, LANES), F32))
        else:
            ref, within = received[e // 9], e % 9
            cells.append(ref[within * 32:within * 32 + 32, :])
    for ref, dz in zip(received, (2, 1, 0)):
        mom = mom + jnp.broadcast_to(ref[MEMBER_ROWS + dz:MEMBER_ROWS + dz + 1, :], (8, LANES))
    for blk in range(7):
        flat = jnp.transpose(jnp.concatenate(cells[blk * 4:blk * 4 + 4], axis=0))
        for c in range(4):
            quads = [flat[c * 32 + q * 8:c * 32 + q * 8 + 8, :] for q in range(4)]
            for a in range(4):
                e = blk * 4 + a
                if e == 27:
                    continue
                mixed = None
                for q in range(4):
                    moved = quads[q] if q == a else pltpu.roll(quads[q], (32 * (q - a)) % 128, 1)
                    mixed = moved if mixed is None else jnp.where(quarter == q, moved, mixed)
                if c < 3:
                    d = (e % 3, e // 3 % 3, e // 9)[c] - 1
                    mixed = mixed + float(TG * d)
                base[c][e * 8:e * 8 + 8, :] = mixed
                base[c][n_rows + e * 8:n_rows + e * 8 + 8, :] = mixed
    for c in range(4):
        v = base[c][0:n_rows, :]
        s1[c, :, :] = pltpu.roll(v, 96, 1)
        s2[c, :, :] = pltpu.roll(v, 64, 1)
    acc[...] = jnp.zeros_like(acc)
    src1 = tuple(s1.at[c] for c in range(4))
    src2 = tuple(s2.at[c] for c in range(4))

    def body(jb, carry):
        at0 = pl.multiple_of(jb * 8, 8)
        for first in (0, 4):
            own = sym_pairs(base, acc, base, at0, first, range(1, 14), skip_self=True, lone=(0,))
            one = sym_pairs(base, acc, src1, at0, first, range(0, 27))
            two = sym_pairs(base, acc, src2, at0, first, range(1, 14), lone=(0,))
            for r in range(4):
                at = pl.ds(at0 + first + r, 1)
                acc[at, :] = acc[at, :] + own[r]
                g1[at, :] = one[r]
                g2[at, :] = two[r]
        return carry

    lax.fori_loop(0, 27, body, 0)
    total = (acc[0:n_rows, :] + acc[n_rows:2 * n_rows, :]
             + pltpu.roll(g1[...], 32, 1) + pltpu.roll(g2[...], 64, 1))
    mass = jnp.sum(m0[0:n_rows, :], axis=0, keepdims=True)
    mass = jnp.broadcast_to(mass, (8, LANES))
    mass = mass + pltpu.roll(mass, 32, 1)
    mass = mass + pltpu.roll(mass, 64, 1)
    mean = mom / mass
    for zs, out in enumerate((out_m, out_0, out_p)):
        out[0:72, :] = total[zs * 72:(zs + 1) * 72, :] * (-GROUP_COUPLING)
        out[72:80, :] = mean


def groups(low, mid, high, after):
    rows = 27 * 8
    return call(group_kernel, [((80, LANES), F32)] * 3, 3,
                [VMEM((2 * rows, LANES), F32)] * 5 + [VMEM((4, rows, LANES), F32)] * 2
                + [VMEM((rows, LANES), F32)] * 2, after=after)(low, mid, high)


def energy_kernel(blocks_ref, low_ref, mid_ref, high_ref, code_ref, vel_ref, bits_ref, keys_ref, out_ref,
                  buf_ref, pot_ref, mean_ref, table_ref, hot_a, hot_b, got_a, got_b):
    received = (low_ref, mid_ref, high_ref)
    rows = bits_ref.shape[0]
    pot_ref[216:256, :] = jnp.zeros((40, LANES), F32)
    mean_ref[216:256, :] = jnp.zeros((40, LANES), F32)
    for cell in range(27):
        ref, within = received[cell // 9], cell % 9
        pot_ref[cell * 8:cell * 8 + 8, :] = ref[within * 16:within * 16 + 8, :]
        mean_ref[cell * 8:cell * 8 + 8, :] = ref[within * 16 + 8:within * 16 + 16, :]
    for k, ref in enumerate((pot_ref, mean_ref)):
        for half in range(2):
            lanes = slice(half * LANES, (half + 1) * LANES)
            flipped = jnp.transpose(ref[lanes, :])
            high = flipped.astype(BF16)
            low = (flipped - high.astype(F32)).astype(BF16)
            base, size = ((0, 128), (256, 96))[k]
            table_ref[base:base + size, lanes] = high[0:size]
            table_ref[base + size:base + 2 * size, lanes] = low[0:size]
    iota_row = lax.broadcasted_iota(I32, (224, LANES), 0).astype(F32).astype(BF16)
    iota_lane = lax.broadcasted_iota(I32, (LANES, LANES), 0)
    iota_group = lax.broadcasted_iota(I32, (32, LANES), 0)
    one_b, zero_b = jnp.ones((224, LANES), BF16), jnp.zeros((224, LANES), BF16)
    hot_a[224:256, :] = jnp.zeros((32, 1024), BF16)
    hot_b[224:256, :] = jnp.zeros((32, 1024), BF16)

    def mark(i, hot_ref):
        at_row = (code_ref[pl.ds(pl.multiple_of(i * 8, 8), 8), :] >> 7).astype(F32)
        for r in range(8):
            lanes = slice(r * LANES, (r + 1) * LANES)
            want = jnp.broadcast_to(at_row[r:r + 1], (224, LANES)).astype(BF16)
            hot_ref[0:224, lanes] = jnp.where(iota_row == want, one_b, zero_b)

    def fetch(i, hot_ref, got_ref):
        here = pl.ds(pl.multiple_of(i * 8, 8), 8)
        code = code_ref[here, :]
        lane = code & 127
        group = code & 31
        for pair in range(4):
            found = jnp.dot(table_ref[...], hot_ref[:, pair * 256:(pair + 1) * 256], preferred_element_type=F32)
            for k in range(2):
                r = pair * 2 + k
                lanes = slice(k * LANES, (k + 1) * LANES)
                pot = found[0:128, lanes] + found[128:256, lanes]
                pot = jnp.where(iota_lane == jnp.broadcast_to(lane[r:r + 1], (LANES, LANES)), pot, 0.0)
                got_ref[0, r:r + 1, :] = jnp.sum(pot, axis=0, keepdims=True)
                at_group = iota_group == jnp.broadcast_to(group[r:r + 1], (32, LANES))
                for c in range(3):
                    o = 256 + c * 32
                    mean = found[o:o + 32, lanes] + found[o + 96:o + 128, lanes]
                    got_ref[1 + c, r:r + 1, :] = jnp.sum(jnp.where(at_group, mean, 0.0), axis=0, keepdims=True)
        kinetic = jnp.zeros((8, LANES), F32)
        for c in range(3):
            diff = vel_ref[c, here, :] - got_ref[1 + c]
            kinetic = kinetic + diff * diff
        buf_ref[pl.ds(pl.multiple_of(i * 8 + 256, 8), 8), :] = got_ref[0] + 0.5 * kinetic

    mark(0, hot_a)

    def gather(i, carry):
        mark(2 * i + 1, hot_b)
        fetch(2 * i, hot_a, got_a)
        mark(2 * i + 2, hot_a)
        fetch(2 * i + 1, hot_b, got_b)
        return carry

    lax.fori_loop(0, (blocks_ref[0] + 1) // 2, gather, 0)
    step_rows = 32
    for stage in reversed(range(STAGES)):
        d = 1 << stage

        def move(i, carry, d=d):
            base = pl.multiple_of((rows // step_rows - 1 - i) * step_rows, step_rows)
            moved = (bits_ref[pl.ds(base, step_rows), :] & d) != 0
            here = pl.ds(pl.multiple_of(base + 256, 8), step_rows)
            buf_ref[here, :] = jnp.where(moved, buf_ref[pl.ds(base + 256 - d, step_rows), :], buf_ref[here, :])
            return carry

        lax.fori_loop(0, rows // step_rows, move, 0)
    out_ref[...] = jnp.where(keys_ref[0:rows, :] < (keys_ref.shape[0] - rows) * LANES * GCAP, buf_ref[pl.ds(256, rows), :], 0.0)


def energies(blocks, low, mid, high, code, vel, bits, table):
    rows = bits.shape[0]
    scratch = [VMEM((rows + 256, LANES), F32), VMEM((256, LANES), F32), VMEM((256, LANES), F32),
               VMEM((448, 256), BF16)] + [VMEM((256, 1024), BF16)] * 2 + [VMEM((4, 8, LANES), F32)] * 2
    return call(energy_kernel, [((rows, LANES), F32)], 8, scratch, smem_first=True)(
        blocks, low, mid, high, code, vel, bits, table)[0]


def up(axis, x):
    n = lax.axis_size(axis)
    return lax.ppermute(x, axis, [(i, (i + 1) % n) for i in range(n)])


def down(axis, x):
    n = lax.axis_size(axis)
    return lax.ppermute(x, axis, [((i + 1) % n, i) for i in range(n)])


def local(particles, labels, member_slot, owner_slot):
    slab_all = particles.shape[-1]
    rows = slab_all // LANES
    parts = particles.reshape(7, rows, LANES)
    keys = labels.reshape(rows, LANES) * GCAP + member_slot.reshape(rows, LANES)
    table = jnp.concatenate([keys, owner_slot.reshape(-1, LANES)], axis=0)
    counts = tuple(lax.axis_size(a) for a in ("gx", "gy", "gz"))
    coords = jnp.stack([lax.axis_index(a) for a in ("gx", "gy", "gz")]).astype(I32)
    send_m, keep, send_p, faces, bits, code, vel, n_blocks = members(coords, counts, table, parts)
    from_low = up("gx", send_p)
    from_high = down("gx", send_m)
    ghost_low = up("gz", faces[3])
    ghost_high = down("gz", faces[2])
    near_xy = near((0, 1), parts, (keep,))
    x_all = (from_low, keep, from_high)

    sums = lax.broadcasted_iota(I32, (8, LANES), 0) < 3

    def stack_y(b):
        mom = sum(t[MEMBER_ROWS + 8 * b:MEMBER_ROWS + 8 * b + 8] for t in x_all)
        return [t[b * 96:(b + 1) * 96] for t in x_all] + [jnp.where(sums, mom, near_xy[0:8])]

    y_low = up("gy", jnp.concatenate(stack_y(2) + [faces[1]], axis=0))
    y_high = down("gy", jnp.concatenate(stack_y(0) + [faces[0]], axis=0))
    y_keep = jnp.concatenate(stack_y(1), axis=0)
    near_z = near((2,), parts, (y_keep,))
    edge_x = far(0, parts, near_xy[0:128], from_low[TOP_X:], from_high[TOP_X:], (y_keep,))
    edge_z = far(2, parts, near_z, ghost_low, ghost_high)
    y_all = (y_low, y_keep, y_high)
    mom_z = sum(t[MEMBER_ROWS:TOP] for t in y_all)
    mom_z = jnp.where(sums, mom_z, edge_x[0:8] + edge_z[0:8])

    def stack_z(b):
        return [t[(3 * xs + b) * 32:(3 * xs + b + 1) * 32] for t in y_all for xs in range(3)] + [mom_z]

    z_low = up("gz", jnp.concatenate(stack_z(2), axis=0))
    z_high = down("gz", jnp.concatenate(stack_z(0), axis=0))
    z_keep = jnp.concatenate(stack_z(1), axis=0)
    edge = far(1, parts, near_xy[128:256], y_low[TOP:], y_high[TOP:], (z_keep,), (edge_x, edge_z))
    to_low, stay, to_high = groups(z_low, z_keep, z_high, (edge,))
    back_high = down("gz", to_low)
    back_low = up("gz", to_high)
    zs = (back_low, stay, back_high)

    def back_y(b):
        return jnp.concatenate([p for t in zs for p in (t[b * 24:(b + 1) * 24], t[72:80])], axis=0)

    ylow = up("gy", back_y(2))
    yhigh = down("gy", back_y(0))
    ys = (ylow, back_y(1), yhigh)

    def back_x(b):
        return jnp.concatenate(
            [p for z in range(3) for t in ys
             for p in (t[z * 32 + b * 8:z * 32 + b * 8 + 8], t[z * 32 + 24:z * 32 + 32])], axis=0)

    xlow = up("gx", back_x(2))
    xhigh = down("gx", back_x(0))
    energy = energies(n_blocks, xlow, back_x(1), xhigh, code, vel, bits, table)
    return edge.reshape(1, 1, 1, slab_all), energy.reshape(1, 1, 1, slab_all)


def solution(mesh):
    return jax.shard_map(
        local,
        mesh=mesh,
        in_specs=(
            P(None, "gx", "gy", "gz", None),
            P("gx", "gy", "gz", None),
            P("gx", "gy", "gz", None),
            P(),
        ),
        out_specs=(P("gx", "gy", "gz", None), P("gx", "gy", "gz", None)),
        check_vma=False,
    )
```
